512 devices in a mesh: replica: 16 (over z_lo, core), fsdp: 32 (over y, z_hi, x).
Axes of the slice: x: 4, y: 4, z: 16 (z_hi: 2, z_lo: 8; z = z_hi * 8 + z_lo), core: 2. Of those that a mesh axis runs over, the one named last changes fastest.
Arguments:
- gradients: bfloat16 [16, 1024, 5120], P('replica', 'fsdp'), may hold values from -150 to 150
- replica_weight: float32 [16], replicated, may hold values from 0.5 to 2
- params: float32 [1024, 5120], P('fsdp'), may hold values from -3 to 3
- first_moment: float32 [1024, 5120], P('fsdp'), may hold values from -3 to 3
- second_moment: float32 [1024, 5120], P('fsdp'), may hold values from 0.05 to 4
Outputs:
- median: float32 [1024, 5120], P('fsdp')
- new_params: float32 [1024, 5120], P('fsdp')
- new_first: float32 [1024, 5120], P('fsdp')
- new_second: float32 [1024, 5120], P('fsdp')
The draws below stay inside these ranges and needn't reach their ends.
All inputs are finite; a program needn't handle non-finite values.
Results may differ from the reference program's by a relative error of at most 0.0003.
Values may be sent and summed in bfloat16 or wider, within the bound.
A program may use at most 64 MiB of HBM per device.

```python
import math
import jax
import jax.numpy as jnp
from jax import lax

D = 5120
ROWS_DEV = 32
ITERS = 4
STEP = 100
REPLICAS = 16
ROWS = 1024


def draw_gradients(key, part):
    key = jax.random.fold_in(key, 11)
    keys = jax.random.split(key, 6)
    position = jnp.arange(ROWS, dtype=jnp.float32) / ROWS
    row_rough = jnp.exp(jax.random.uniform(keys[0], (ROWS,), jnp.float32, jnp.log(0.5), jnp.log(2.0)))
    col_scale = jnp.exp(jax.random.uniform(keys[1], (D,), jnp.float32, jnp.log(0.3), jnp.log(3.0)))
    base_sigma = jnp.exp(jax.random.uniform(keys[4], (REPLICAS,), jnp.float32, jnp.log(0.01), jnp.log(1.0)))
    block_rows = ROWS_DEV // REPLICAS
    block_count = ROWS // block_rows
    block_factor = jnp.exp(jax.random.uniform(keys[5], (REPLICAS, block_count), jnp.float32, jnp.log(0.25), jnp.log(2.5)))
    sigma_rows = jnp.broadcast_to((base_sigma[:, None] * block_factor)[:, :, None], (REPLICAS, block_count, block_rows)).reshape(REPLICAS, ROWS)
    row_scale = 3.0 ** (position - 0.5) * row_rough
    common = jnp.clip(jax.random.normal(keys[2], (ROWS, D), jnp.float32), -4.0, 4.0)
    noise = jnp.clip(jax.random.normal(keys[3], (REPLICAS, ROWS, D), jnp.float32), -4.0, 4.0)
    values = (common[None] + sigma_rows[:, :, None] * noise) * row_scale[None, :, None] * col_scale[None, None, :]
    return values.astype(jnp.bfloat16)


def levels(stream_key, shape, shards, least, largest):
    def one(dim, shards_of):
        draws = jax.random.uniform(jax.random.fold_in(jax.random.fold_in(stream_key, 6), dim), (shards_of,), jnp.float32, least / len(shards), largest / len(shards))
        return jnp.repeat(jnp.exp(draws), shape[dim] // shards_of).reshape((-1,) + (1,) * (len(shape) - dim - 1))

    factor_of = one(*shards[0])
    for cut in shards[1:]:
        factor_of = factor_of * one(*cut)
    return factor_of


def scatter_about(rng, shape, scale, most, cuts=(), kind=jnp.bfloat16):
    values = jax.random.normal(rng, shape, jnp.float32) * scale
    if len(cuts) > 0:
        values = levels(rng, shape, cuts, -0.22, 0.18) * values
    return jnp.clip(values, min=-most, max=most).astype(kind)


def setup_inputs(seed: int = 0) -> dict:
    key_list = jax.random.split(jax.random.key(seed), 6)
    gradients = draw_gradients(jax.random.fold_in(key_list[5], 71), 0)
    replica_weight = jnp.clip(jnp.exp(jax.random.uniform(key_list[1], (REPLICAS,), jnp.float32, math.log(0.5), math.log(2.0))), 0.5, 2.0)
    params = scatter_about(key_list[2], (ROWS, D), 0.5, 3.0, ((0, 32),), jnp.float32)
    first_moment = scatter_about(key_list[3], (ROWS, D), 0.5, 3.0, ((0, 32),), jnp.float32)
    second_moment = jnp.clip(jnp.exp(math.log(4.0) - 4.3820266 * jax.random.uniform(key_list[4], (ROWS, D), jnp.float32) ** levels(key_list[4], (ROWS, D), ((0, 32),), -0.2, 0.2)), 0.05, 4.0)
    return {"gradients": gradients, "replica_weight": replica_weight, "params": params, "first_moment": first_moment, "second_moment": second_moment}


smooth_floor = 0.05
beta_first = 0.9
beta_second = 0.95
learn_rate = 0.001
decay_rate = 0.1
adam_epsilon = 1e-08

def pool_rows(weights, gradients):
    weighted = jnp.einsum('r,rij->ij', weights.astype(jnp.float32), gradients.astype(jnp.float32), precision=lax.Precision.HIGHEST)
    return weighted / jnp.sum(weights)

def reference(gradients, replica_weight, params, first_moment, second_moment):
    entries = ROWS * D
    median = pool_rows(replica_weight, gradients)
    for iteration in range(ITERS):
        partials = lax.optimization_barrier(jnp.sum(jnp.square(gradients.astype(jnp.float32) - median[None]), axis=(1, 2)))
        distance = jnp.sqrt(partials / entries)
        median = pool_rows(replica_weight / jnp.maximum(distance, smooth_floor), gradients)
    new_first = beta_first * first_moment + (1.0 - beta_first) * median
    new_second = beta_second * second_moment + (1.0 - beta_second) * median * median
    first_hat = new_first / (1.0 - beta_first ** STEP)
    second_hat = new_second / (1.0 - beta_second ** STEP)
    new_params = params - learn_rate * (first_hat / (jnp.sqrt(second_hat) + adam_epsilon) + decay_rate * params)
    return (median, new_params, new_first, new_second)
```

```python
import functools

import jax
import jax.numpy as jnp
from jax import lax
from jax.experimental import pallas as pl
from jax.experimental.pallas import tpu as pltpu
from jax.sharding import PartitionSpec as P

ITERS = 4
STEP = 100

smooth_floor = 0.05
beta_first = 0.9
beta_second = 0.95
learn_rate = 0.001
decay_rate = 0.1
adam_epsilon = 1e-08

MESH = pl.DeviceIdType.MESH
LANES = 128


def packed_gram(block, groups, rows):
    product = lax.dot_general(block, block, (((1,), (1,)), ((), ())), preferred_element_type=jnp.float32)
    size = groups * rows
    row = lax.broadcasted_iota(jnp.int32, (size, size), 0)
    column = lax.broadcasted_iota(jnp.int32, (size, size), 1)
    same = lax.rem(row, rows) == lax.rem(column, rows)
    by_group = jnp.sum(jnp.where(same, product, 0.0).reshape(groups, rows, size), axis=1)
    lane = lax.broadcasted_iota(jnp.int32, (groups, LANES), 1)
    low, high = by_group[:, :LANES], by_group[:, LANES:]
    low, high = low + pltpu.roll(low, LANES - 8, 1), high + pltpu.roll(high, 8, 1)
    half = jnp.where(lax.rem(lane, 16) < 8, low, high)
    low, high = half[:8], half[8:]
    low, high = low + pltpu.roll(low, LANES - 4, 1), high + pltpu.roll(high, 4, 1)
    return jnp.where(lax.rem(lane[:8], 8) < 4, low, high)


def median_weights(packed, weight_ref, groups, entries):
    lane = lax.broadcasted_iota(jnp.int32, (groups, LANES), 1)
    sub = lax.broadcasted_iota(jnp.int32, (groups, LANES), 0)
    lane_group = lax.div(lane, 16) + 8 * lax.div(lax.rem(lane, 16), 8)
    here = lax.div(lax.rem(lane, 8), 4) == lax.div(sub, 8)
    gram = jnp.where(here, jnp.concatenate([packed, packed], axis=0), 0.0) * (1.0 / entries)
    own_lane = lane_group == sub
    given = jnp.zeros((groups, LANES), jnp.float32)
    for group in range(groups):
        given = jnp.where(sub == group, weight_ref[group], given)
    norm = jnp.sum(jnp.where(own_lane, gram, 0.0), axis=1, keepdims=True)
    weight = given
    for iteration in range(ITERS + 1):
        weight = weight / jnp.sum(weight, axis=0, keepdims=True)
        if iteration == ITERS:
            break
        along_lanes = jnp.sum(jnp.where(own_lane, weight, 0.0), axis=0, keepdims=True)
        product = jnp.sum(gram * along_lanes, axis=1, keepdims=True)
        squared = norm - 2.0 * product + jnp.sum(weight * product, axis=0, keepdims=True)
        weight = given / jnp.maximum(jnp.sqrt(jnp.maximum(squared, 0.0)), smooth_floor)
    return weight


def kernel(
    groups, row_parts, entries, grad_ref, weight_ref, out_ref, held, small, first_slots, second_slots,
    here_sem, held_send, held_recv, first_send, first_recv, second_send, second_recv,
    chip_send, chip_recv, core_send, core_recv,
):
    replica = lax.axis_index("replica")
    fsdp = lax.axis_index("fsdp")
    chips = groups // 2
    chip, core = lax.div(replica, 2), lax.rem(replica, 2)
    rows = grad_ref.shape[0] // 2
    wide = grad_ref.shape[1] // chips

    def peer(distance):
        return lax.rem(replica + distance, groups)

    def row_peer(distance):
        return lax.rem(fsdp + distance, row_parts)

    barrier = pltpu.get_barrier_semaphore()

    @pl.loop(1, groups)
    def _(distance):
        pl.semaphore_signal(barrier, inc=1, device_id={"replica": peer(distance)}, device_id_type=MESH)

    @pl.loop(1, row_parts)
    def _(distance):
        pl.semaphore_signal(barrier, inc=1, device_id={"fsdp": row_peer(distance)}, device_id_type=MESH)

    pl.semaphore_wait(barrier, groups - 1 + row_parts - 1)

    def part_of(ref, owner_chip, owner_core):
        return ref.at[
            pl.ds(pl.multiple_of(owner_core * rows, rows), rows),
            pl.ds(pl.multiple_of(owner_chip * wide, wide), wide),
        ]

    def held_slot(group):
        return held.at[pl.ds(pl.multiple_of(group * rows, rows), rows), :]

    @pl.loop(1, groups)
    def _(distance):
        to = peer(distance)
        pltpu.make_async_remote_copy(
            src_ref=part_of(grad_ref, lax.div(to, 2), lax.rem(to, 2)),
            dst_ref=held_slot(replica),
            send_sem=held_send,
            recv_sem=held_recv,
            device_id={"replica": to},
            device_id_type=MESH,
        ).start()

    pltpu.make_async_copy(part_of(grad_ref, chip, core), held_slot(replica), held_recv).start()
    pltpu.make_async_copy(held, held, held_recv).wait()

    small[...] = packed_gram(held[...], groups, rows)

    @pl.loop(1, groups)
    def _(distance):
        pltpu.make_async_remote_copy(
            src_ref=small,
            dst_ref=first_slots.at[replica],
            send_sem=first_send,
            recv_sem=first_recv,
            device_id={"replica": peer(distance)},
            device_id_type=MESH,
        ).start()

    pltpu.make_async_copy(small, first_slots.at[replica], first_recv).start()
    pltpu.make_async_copy(first_slots, first_slots, first_recv).wait()
    rest = first_slots.at[pl.ds(0, groups - 1)]
    pltpu.make_async_copy(rest, rest, first_send).wait()
    small[...] = jnp.sum(first_slots[...], axis=0)

    @pl.loop(1, row_parts)
    def _(distance):
        pltpu.make_async_remote_copy(
            src_ref=small,
            dst_ref=second_slots.at[fsdp],
            send_sem=second_send,
            recv_sem=second_recv,
            device_id={"fsdp": row_peer(distance)},
            device_id_type=MESH,
        ).start()

    pltpu.make_async_copy(small, second_slots.at[fsdp], second_recv).start()
    pltpu.make_async_copy(second_slots, second_slots, second_recv).wait()
    weights = median_weights(jnp.sum(second_slots[...], axis=0), weight_ref, groups, entries)

    total = jnp.zeros((rows, wide), jnp.float32)
    for group in range(groups):
        total += weights[group : group + 1, :1] * held[group * rows : (group + 1) * rows, :].astype(jnp.float32)
    part_of(out_ref, chip, core)[...] = total

    sibling = {"replica": chip * 2 + 1 - core}
    beside = chip + 1 - 2 * lax.rem(chip, 2)
    parity = lax.rem(chip, 2)
    pairs = chips // 2

    def to_chip(from_chip, target):
        return pltpu.make_async_remote_copy(
            src_ref=part_of(out_ref, from_chip, core),
            dst_ref=part_of(out_ref, from_chip, core),
            send_sem=chip_send.at[from_chip],
            recv_sem=chip_recv.at[from_chip],
            device_id={"replica": target * 2 + core},
            device_id_type=MESH,
        )

    def to_core(from_chip, from_core):
        return pltpu.make_async_remote_copy(
            src_ref=part_of(out_ref, from_chip, from_core),
            dst_ref=part_of(out_ref, from_chip, from_core),
            send_sem=core_send.at[from_chip],
            recv_sem=core_recv.at[from_chip],
            device_id=sibling,
            device_id_type=MESH,
        )

    def far(step):
        return lax.rem(lax.div(chip, 2) + step, pairs) * 2 + parity

    for step in range(1, pairs):
        pltpu.make_async_remote_copy(
            src_ref=part_of(out_ref, chip, core),
            dst_ref=part_of(out_ref, chip, core),
            send_sem=here_sem.at[step],
            recv_sem=chip_recv.at[chip],
            device_id={"replica": far(step) * 2 + core},
            device_id_type=MESH,
        ).start()
    to_chip(chip, beside).start()
    to_core(chip, core).start()

    for step in range(1, pairs):
        origin = far(pairs - step)
        to_chip(origin, beside).wait_recv()
        to_chip(origin, beside).start()
        to_core(origin, core).start()
    for step in range(pairs):
        origin = lax.rem(lax.div(chip, 2) + step, pairs) * 2 + 1 - parity
        to_chip(origin, beside).wait_recv()
        to_core(origin, core).start()
    for origin in range(chips):
        to_core(origin, 1 - core).wait_recv()

    for origin in range(chips):
        to_core(origin, core).wait_send()
    for step in range(pairs):
        to_chip(far(step), beside).wait_send()
    for step in range(1, pairs):
        pltpu.make_async_remote_copy(
            src_ref=part_of(out_ref, chip, core),
            dst_ref=part_of(out_ref, chip, core),
            send_sem=here_sem.at[step],
            recv_sem=chip_recv.at[chip],
            device_id={"replica": far(step) * 2 + core},
            device_id_type=MESH,
        ).wait_send()
    sent = held.at[pl.ds(0, (groups - 1) * rows), :]
    pltpu.make_async_copy(sent, sent, held_send).wait()
    rest = second_slots.at[pl.ds(0, row_parts - 1)]
    pltpu.make_async_copy(rest, rest, second_send).wait()


def body(groups, row_parts, gradients, replica_weight, params, first_moment, second_moment):
    rows_here, width = gradients.shape[1], gradients.shape[2]
    entries = rows_here * row_parts * width
    rows, wide, half = rows_here // 2, width // (groups // 2), groups // 2
    dma = pltpu.SemaphoreType.DMA
    median = pl.pallas_call(
        functools.partial(kernel, groups, row_parts, entries),
        out_shape=jax.ShapeDtypeStruct((rows_here, width), jnp.float32),
        in_specs=[pl.BlockSpec(memory_space=pl.ANY), pl.BlockSpec(memory_space=pltpu.SMEM)],
        out_specs=pl.BlockSpec(memory_space=pltpu.VMEM),
        scratch_shapes=[
            pltpu.VMEM((groups * rows, wide), jnp.bfloat16),
            pltpu.VMEM((half, LANES), jnp.float32),
            pltpu.VMEM((groups, half, LANES), jnp.float32),
            pltpu.VMEM((row_parts, half, LANES), jnp.float32),
            dma((half // 2,)),
            dma, dma, dma, dma, dma, dma,
            dma((half,)), dma((half,)), dma((half,)), dma((half,)),
        ],
        compiler_params=pltpu.CompilerParams(collective_id=0, has_side_effects=True),
        name="median_rows",
    )(gradients.reshape(rows_here, width), replica_weight)
    new_first = beta_first * first_moment + (1.0 - beta_first) * median
    new_second = beta_second * second_moment + (1.0 - beta_second) * median * median
    first_hat = new_first / (1.0 - beta_first**STEP)
    second_hat = new_second / (1.0 - beta_second**STEP)
    new_params = params - learn_rate * (
        first_hat / (jnp.sqrt(second_hat) + adam_epsilon) + decay_rate * params
    )
    return (median, new_params, new_first, new_second)


def solution(mesh):
    return jax.shard_map(
        functools.partial(body, mesh.shape["replica"], mesh.shape["fsdp"]),
        mesh=mesh,
        in_specs=(
            P("replica", "fsdp", None),
            P(),
            P("fsdp", None),
            P("fsdp", None),
            P("fsdp", None),
        ),
        out_specs=(P("fsdp", None), P("fsdp", None), P("fsdp", None), P("fsdp", None)),
        check_vma=False,
    )
```

```python
import functools
import math

import jax
import jax.numpy as jnp
from jax import lax
from jax.experimental import pallas as pl
from jax.experimental.pallas import tpu as pltpu
from jax.sharding import PartitionSpec as P

ITERS = 4
STEP = 100

smooth_floor = 0.05
beta_first = 0.9
beta_second = 0.95
learn_rate = 0.001
decay_rate = 0.1
adam_epsilon = 1e-08

MESH = pl.DeviceIdType.MESH
LANES = 128


def packed_gram(block, groups, rows):
    product = lax.dot_general(block, block, (((1,), (1,)), ((), ())), preferred_element_type=jnp.float32)
    size = groups * rows
    row = lax.broadcasted_iota(jnp.int32, (size, size), 0)
    column = lax.broadcasted_iota(jnp.int32, (size, size), 1)
    same = lax.rem(row, rows) == lax.rem(column, rows)
    by_group = jnp.sum(jnp.where(same, product, 0.0).reshape(groups, rows, size), axis=1)
    lane = lax.broadcasted_iota(jnp.int32, (groups, LANES), 1)

    def fold(low, high, step):
        low, high = low + pltpu.roll(low, LANES - step, 1), high + pltpu.roll(high, step, 1)
        return jnp.where(lax.rem(lane[: low.shape[0]], 2 * step) < step, low, high)

    folded = fold(by_group[:, :LANES], by_group[:, LANES:], 8)
    folded = fold(folded[:8], folded[8:], 4)
    folded = fold(folded[:4], folded[4:], 2)
    return fold(folded[:2], folded[2:], 1)


def median_weights(packed, weight_ref, groups, entries):
    lane = lax.broadcasted_iota(jnp.int32, (groups, LANES), 1)
    sub = lax.broadcasted_iota(jnp.int32, (groups, LANES), 0)
    lane_group = lax.div(lane, 16) + 8 * lax.div(lax.rem(lane, 16), 8)
    here = lax.rem(lane, 8) == lax.div(sub, 2)
    both = jnp.where(lax.rem(sub, 2) == 0, packed[:1], packed[1:])
    gram = jnp.where(here, both, 0.0) * (1.0 / entries)
    own_lane = lane_group == sub
    given = jnp.zeros((groups, LANES), jnp.float32)
    for group in range(groups):
        given = jnp.where(sub == group, weight_ref[group], given)
    norm = jnp.sum(jnp.where(own_lane, gram, 0.0), axis=1, keepdims=True)
    weight = given
    for iteration in range(ITERS + 1):
        weight = weight / jnp.sum(weight, axis=0, keepdims=True)
        if iteration == ITERS:
            break
        along_lanes = jnp.sum(jnp.where(own_lane, weight, 0.0), axis=0, keepdims=True)
        product = jnp.sum(gram * along_lanes, axis=1, keepdims=True)
        squared = norm - 2.0 * product + jnp.sum(weight * product, axis=0, keepdims=True)
        weight = given / jnp.maximum(jnp.sqrt(jnp.maximum(squared, 0.0)), smooth_floor)
    return weight


def kernel(
    chips, grid, entries, grad_ref, weight_hbm, params_hbm, first_hbm, second_hbm,
    out_ref, params_ref, first_ref, second_ref,
    weight_ref, held, core_small, plane_small, ring_small, core_slot, plane_slots, ring_slots,
    up, down, beside_sem, near_row, next_row, far_row,
    weight_sem, copy_sem, held_send, held_recv, core_sem, core_sum_recv,
    plane_send, plane_recv, ring_send, ring_recv,
    far_send, chip_send, chip_recv, core_send, core_recv,
):
    rows_y, runs, rows_x = grid
    groups, plane, ring = 2 * chips, rows_x * rows_y, runs * chips
    replica, fsdp = lax.axis_index("replica"), lax.axis_index("fsdp")
    chip, core = lax.div(replica, 2), lax.rem(replica, 2)
    x, run, y = lax.rem(fsdp, rows_x), lax.rem(lax.div(fsdp, rows_x), runs), lax.div(fsdp, rows_x * runs)
    z = run * chips + chip
    rows = grad_ref.shape[0] // 2
    wide = grad_ref.shape[1] // chips

    def device(dz=0, dy=0, dx=0, other=False):
        to_z = lax.rem(z + dz + ring, ring)
        to_y = lax.rem(y + dy + rows_y, rows_y)
        to_x = lax.rem(x + dx + rows_x, rows_x)
        return {
            "replica": lax.rem(to_z, chips) * 2 + (1 - core if other else core),
            "fsdp": (to_y * runs + lax.div(to_z, chips)) * rows_x + to_x,
        }

    def steps(size):
        return {1: (), 2: (1,)}.get(size, (1, -1))

    def tell(sem, to):
        pl.semaphore_signal(sem, inc=1, device_id=to, device_id_type=MESH)

    def send(src, dst, send_sem, recv_sem, to):
        return pltpu.make_async_remote_copy(
            src_ref=src, dst_ref=dst, send_sem=send_sem, recv_sem=recv_sem, device_id=to, device_id_type=MESH
        )

    def await_bytes(ref, sem):
        pltpu.make_async_copy(ref, ref, sem).wait()

    weight_copy = pltpu.make_async_copy(weight_hbm, weight_ref, weight_sem)
    weight_copy.start()

    barrier = pltpu.get_barrier_semaphore()
    greeted = [device(dz=dz, other=other) for dz in steps(ring) for other in (False, True)]
    greeted += [device(dy=dy) for dy in steps(rows_y)] + [device(dx=dx) for dx in steps(rows_x)]
    greeted += [device(other=True)]
    for to in greeted:
        tell(barrier, to)
    pl.semaphore_wait(barrier, len(greeted))

    def part_of(ref, owner_chip, owner_core):
        return ref.at[
            pl.ds(pl.multiple_of(owner_core * rows, rows), rows),
            pl.ds(pl.multiple_of(owner_chip * wide, wide), wide),
        ]

    own_held = held.at[pl.ds(pl.multiple_of(replica * rows, rows), rows), :]

    def send_part(to_chip, to_core):
        to = {"replica": to_chip * 2 + to_core}
        send(part_of(grad_ref, to_chip, to_core), own_held, held_send, held_recv, to).start()

    send_part(chip, 1 - core)
    pltpu.make_async_copy(part_of(grad_ref, chip, core), own_held, held_recv).start()

    for distance in range(1, ring // 2 + 1):
        if distance > 1:
            pl.semaphore_wait(up.at[distance], 1)
            if 2 * distance < ring:
                pl.semaphore_wait(down.at[distance], 1)
        if distance < ring // 2:
            tell(up.at[distance + 1], device(dz=1))
            if 2 * distance + 2 < ring:
                tell(down.at[distance + 1], device(dz=-1))
        if distance < chips:
            @pl.when(chip + distance < chips)
            def _():
                send_part(chip + distance, core)
                send_part(chip + distance, 1 - core)

            @pl.when(chip >= distance)
            def _():
                send_part(chip - distance, core)
                send_part(chip - distance, 1 - core)

    if rows_x > 2:
        tell(beside_sem, device(dx=1))
        pl.semaphore_wait(beside_sem, 1)
    for dy in steps(rows_y):
        tell(near_row if dy == 1 else next_row, device(dy=dy))
    for dy in steps(rows_y):
        pl.semaphore_wait(near_row if dy == 1 else next_row, 1)
    if rows_y > 2:
        tell(far_row, device(dy=1))
        pl.semaphore_wait(far_row, 1)

    kept = [
        pltpu.make_async_copy(params_hbm, params_ref, copy_sem.at[0]),
        pltpu.make_async_copy(first_hbm, first_ref, copy_sem.at[1]),
        pltpu.make_async_copy(second_hbm, second_ref, copy_sem.at[2]),
    ]
    for copy in kept:
        copy.start()
    weight_copy.wait()

    await_bytes(held, held_recv)
    core_small[...] = packed_gram(held[...], groups, rows)

    exchange = send(core_small, core_slot, core_sem, core_sum_recv, device(other=True))
    exchange.start()
    exchange.wait()
    plane_small[...] = core_small[...] + core_slot[...]

    if plane > 1:
        for step in range(1, plane):
            to = device(dx=step % rows_x, dy=step // rows_x)
            send(plane_small, plane_slots.at[y * rows_x + x], plane_send, plane_recv, to).start()
        pltpu.make_async_copy(plane_small, plane_slots.at[y * rows_x + x], plane_recv).start()
        await_bytes(plane_slots, plane_recv)
        ring_small[...] = jnp.sum(plane_slots[...], axis=0)
    else:
        ring_small[...] = plane_small[...]

    for step in range(1, ring):
        send(ring_small, ring_slots.at[z], ring_send, ring_recv, device(dz=step)).start()
    pltpu.make_async_copy(ring_small, ring_slots.at[z], ring_recv).start()
    await_bytes(ring_slots, ring_recv)
    weights = median_weights(jnp.sum(ring_slots[...], axis=0), weight_ref, groups, entries)

    total = jnp.zeros((rows, wide), jnp.float32)
    for group in range(groups):
        total += weights[group : group + 1, :1] * held[group * rows : (group + 1) * rows, :].astype(jnp.float32)
    part_of(out_ref, chip, core)[...] = total

    sibling = {"replica": chip * 2 + 1 - core}
    beside = chip + 1 - 2 * lax.rem(chip, 2)
    parity = lax.rem(chip, 2)
    pairs = chips // 2

    def far(step):
        return lax.rem(lax.div(chip, 2) + step, pairs) * 2 + parity

    def to_chip(origin, target, send_sem):
        part = part_of(out_ref, origin, core)
        return send(part, part, send_sem, chip_recv.at[origin], {"replica": target * 2 + core})

    def to_core(origin, origin_core):
        part = part_of(out_ref, origin, origin_core)
        return send(part, part, core_send.at[origin], core_recv.at[origin], sibling)

    for step in range(1, pairs):
        to_chip(chip, far(step), far_send.at[step]).start()
    to_chip(chip, beside, chip_send.at[chip]).start()
    to_core(chip, core).start()
    for step in range(1, pairs):
        origin = far(pairs - step)
        to_chip(origin, beside, chip_send.at[origin]).wait_recv()
        to_chip(origin, beside, chip_send.at[origin]).start()
        to_core(origin, core).start()
    for step in range(pairs):
        origin = far(step) + 1 - 2 * parity
        to_chip(origin, beside, chip_send.at[origin]).wait_recv()
        to_core(origin, core).start()
    for origin in range(chips):
        to_core(origin, 1 - core).wait_recv()

    for origin in range(chips):
        to_core(origin, core).wait_send()
    for step in range(pairs):
        to_chip(far(step), beside, chip_send.at[far(step)]).wait_send()
    for step in range(1, pairs):
        to_chip(chip, far(step), far_send.at[step]).wait_send()
    for copy in kept:
        copy.wait()
    await_bytes(held.at[pl.ds(0, (groups - 1) * rows), :], held_send)
    if plane > 1:
        await_bytes(plane_slots.at[pl.ds(0, plane - 1)], plane_send)
    await_bytes(ring_slots.at[pl.ds(0, ring - 1)], ring_send)


def update_kernel(
    median_ref, params_ref, first_ref, second_ref, median_hbm, params_hbm, first_hbm, second_hbm,
    params_new, first_new, second_new, median_sem, sems,
):
    median_copy = pltpu.make_async_copy(median_ref, median_hbm, median_sem)
    median_copy.start()
    rows, width = median_ref.shape
    cut = 8
    copies = []
    for part in range(rows // cut):
        at = pl.ds(part * cut, cut)
        median = median_ref[at, :]
        new_first = beta_first * first_ref[at, :] + (1.0 - beta_first) * median
        new_second = beta_second * second_ref[at, :] + (1.0 - beta_second) * median * median
        first_hat = new_first / (1.0 - beta_first**STEP)
        second_hat = new_second / (1.0 - beta_second**STEP)
        params = params_ref[at, :]
        params_new[at, :] = params - learn_rate * (
            first_hat / (jnp.sqrt(second_hat) + adam_epsilon) + decay_rate * params
        )
        first_new[at, :] = new_first
        second_new[at, :] = new_second
        for kind, (new, hbm) in enumerate(
            ((params_new, params_hbm), (first_new, first_hbm), (second_new, second_hbm))
        ):
            copy = pltpu.make_async_copy(new.at[at, :], hbm.at[at, :], sems.at[part, kind])
            copy.start()
            copies.append(copy)
    for copy in copies:
        copy.wait()
    median_copy.wait()


def body(chips, grid, gradients, replica_weight, params, first_moment, second_moment):
    rows_here, width = gradients.shape[1], gradients.shape[2]
    rows_y, runs, rows_x = grid
    groups, ring = 2 * chips, runs * chips
    entries = rows_here * rows_y * runs * rows_x * width
    rows, wide = rows_here // 2, width // chips
    dma, regular = pltpu.SemaphoreType.DMA, pltpu.SemaphoreType.REGULAR
    whole = jax.ShapeDtypeStruct((rows_here, width), jnp.float32)
    in_hbm = pl.BlockSpec(memory_space=pltpu.HBM)
    in_vmem = pl.BlockSpec(memory_space=pltpu.VMEM)
    small = pltpu.VMEM((2, LANES), jnp.float32)
    gathered = pl.pallas_call(
        functools.partial(kernel, chips, grid, entries),
        out_shape=(whole,) * 4,
        in_specs=[in_hbm] * 5,
        out_specs=(in_vmem,) * 4,
        scratch_shapes=[
            pltpu.SMEM((groups,), jnp.float32),
            pltpu.VMEM((groups * rows, wide), jnp.bfloat16),
            small, small, small, small,
            pltpu.VMEM((rows_x * rows_y, 2, LANES), jnp.float32),
            pltpu.VMEM((ring, 2, LANES), jnp.float32),
            regular((ring // 2 + 1,)), regular((ring // 2 + 1,)), regular, regular, regular, regular,
            dma, dma((3,)), dma, dma, dma, dma,
            dma, dma, dma, dma,
            dma((chips // 2,)), dma((chips,)), dma((chips,)), dma((chips,)), dma((chips,)),
        ],
        compiler_params=pltpu.CompilerParams(collective_id=0, has_side_effects=True, vmem_limit_bytes=51 * 1024 * 1024),
        name="median_rows",
    )(gradients.reshape(rows_here, width), replica_weight, params, first_moment, second_moment)
    kept = pltpu.VMEM((rows_here, width), jnp.float32)
    return pl.pallas_call(
        update_kernel,
        out_shape=(whole,) * 4,
        in_specs=[in_vmem] * 4,
        out_specs=(in_hbm,) * 4,
        scratch_shapes=[kept, kept, kept, dma, dma((rows_here // 8, 3))],
        compiler_params=pltpu.CompilerParams(vmem_limit_bytes=16 * 1024 * 1024),
        name="update",
    )(*gathered)


def solution(mesh):
    chips = mesh.shape["replica"] // 2
    side = math.isqrt(mesh.shape["fsdp"] // 2)
    return jax.shard_map(
        functools.partial(body, chips, (side, 2, side)),
        mesh=mesh,
        in_specs=(
            P("replica", "fsdp", None),
            P(),
            P("fsdp", None),
            P("fsdp", None),
            P("fsdp", None),
        ),
        out_specs=(P("fsdp", None), P("fsdp", None), P("fsdp", None), P("fsdp", None)),
        check_vma=False,
    )
```

```python
import functools
import math

import jax
import jax.numpy as jnp
from jax import lax
from jax.experimental import pallas as pl
from jax.experimental.pallas import tpu as pltpu
from jax.sharding import PartitionSpec as P

ITERS = 4
STEP = 100

smooth_floor = 0.05
beta_first = 0.9
beta_second = 0.95
learn_rate = 0.001
decay_rate = 0.1
adam_epsilon = 1e-08

MESH = pl.DeviceIdType.MESH
LANES = 128
PIECES = 1
GATHER = ({4: 0, 2: 0, 1: 0, 3: 0, 6: 4, 5: 4, 7: 4}, 1)


def depth_of(tree, offset):
    return 0 if offset == 0 else 1 + depth_of(tree, tree[offset])


def packed_gram(block, groups, rows):
    product = lax.dot_general(block, block, (((1,), (1,)), ((), ())), preferred_element_type=jnp.float32)
    size = groups * rows
    row = lax.broadcasted_iota(jnp.int32, (size, size), 0)
    column = lax.broadcasted_iota(jnp.int32, (size, size), 1)
    same = lax.rem(row, rows) == lax.rem(column, rows)
    by_group = jnp.sum(jnp.where(same, product, 0.0).reshape(groups, rows, size), axis=1)
    lane = lax.broadcasted_iota(jnp.int32, (groups, LANES), 1)

    def fold(low, high, step):
        low, high = low + pltpu.roll(low, LANES - step, 1), high + pltpu.roll(high, step, 1)
        return jnp.where(lax.rem(lane[: low.shape[0]], 2 * step) < step, low, high)

    folded = fold(by_group[:, :LANES], by_group[:, LANES:], 8)
    folded = fold(folded[:8], folded[8:], 4)
    folded = fold(folded[:4], folded[4:], 2)
    return fold(folded[:2], folded[2:], 1)


def median_weights(packed, weight_ref, groups, entries):
    lane = lax.broadcasted_iota(jnp.int32, (groups, LANES), 1)
    sub = lax.broadcasted_iota(jnp.int32, (groups, LANES), 0)
    lane_group = lax.div(lane, 16) + 8 * lax.div(lax.rem(lane, 16), 8)
    here = lax.rem(lane, 8) == lax.div(sub, 2)
    both = jnp.where(lax.rem(sub, 2) == 0, packed[:1], packed[1:])
    gram = jnp.where(here, both, 0.0) * (1.0 / entries)
    own_lane = lane_group == sub
    given = jnp.zeros((groups, LANES), jnp.float32)
    for group in range(groups):
        given = jnp.where(sub == group, weight_ref[group], given)
    norm = jnp.sum(jnp.where(own_lane, gram, 0.0), axis=1, keepdims=True)
    weight = given
    for iteration in range(ITERS + 1):
        weight = weight / jnp.sum(weight, axis=0, keepdims=True)
        if iteration == ITERS:
            break
        along_lanes = jnp.sum(jnp.where(own_lane, weight, 0.0), axis=0, keepdims=True)
        product = jnp.sum(gram * along_lanes, axis=1, keepdims=True)
        squared = norm - 2.0 * product + jnp.sum(weight * product, axis=0, keepdims=True)
        weight = given / jnp.maximum(jnp.sqrt(jnp.maximum(squared, 0.0)), smooth_floor)
    return weight


def kernel(
    chips, grid, entries, grad_hbm, weight_hbm, params_hbm, first_hbm, second_hbm,
    out_ref, params_ref, first_ref, second_ref,
    grad_ref, weight_ref, held, core_small, plane_small, ring_small, core_slot, plane_slots, ring_slots,
    reached, beside_sem, near_row, next_row, far_row,
    grad_sem, weight_sem, copy_sem, held_send, held_recv, core_sem, core_sum_recv,
    plane_send, plane_recv, ring_send, ring_recv,
    chip_send, chip_recv, core_send, core_recv,
):
    rows_y, runs, rows_x = grid
    groups, plane, ring = 2 * chips, rows_x * rows_y, runs * chips
    replica, fsdp = lax.axis_index("replica"), lax.axis_index("fsdp")
    chip, core = lax.div(replica, 2), lax.rem(replica, 2)
    x, run, y = lax.rem(fsdp, rows_x), lax.rem(lax.div(fsdp, rows_x), runs), lax.div(fsdp, rows_x * runs)
    z = run * chips + chip
    rows = grad_ref.shape[0] // 2
    wide = grad_ref.shape[1] // chips

    def device(dz=0, dy=0, dx=0, other=False):
        to_z = lax.rem(z + dz + ring, ring)
        to_y = lax.rem(y + dy + rows_y, rows_y)
        to_x = lax.rem(x + dx + rows_x, rows_x)
        return {
            "replica": lax.rem(to_z, chips) * 2 + (1 - core if other else core),
            "fsdp": (to_y * runs + lax.div(to_z, chips)) * rows_x + to_x,
        }

    def hops(step, size):
        return min(step, size - step)

    def steps(size):
        return {1: (), 2: (1,)}.get(size, (1, -1))

    def tell(sem, to):
        pl.semaphore_signal(sem, inc=1, device_id=to, device_id_type=MESH)

    def send(src, dst, send_sem, recv_sem, to):
        return pltpu.make_async_remote_copy(
            src_ref=src, dst_ref=dst, send_sem=send_sem, recv_sem=recv_sem, device_id=to, device_id_type=MESH
        )

    def await_bytes(ref, sem):
        pltpu.make_async_copy(ref, ref, sem).wait()

    grad_copy = pltpu.make_async_copy(grad_hbm, grad_ref, grad_sem)
    grad_copy.start()
    weight_copy = pltpu.make_async_copy(weight_hbm, weight_ref, weight_sem)
    weight_copy.start()

    barrier = pltpu.get_barrier_semaphore()
    greeted = [device(dz=dz, other=other) for dz in (-2, -1, 1, 2) for other in (False, True)]
    greeted += [device(dy=dy) for dy in steps(rows_y)] + [device(dx=dx) for dx in steps(rows_x)]
    greeted += [device(other=True)]
    for to in greeted:
        tell(barrier, to)
    pl.semaphore_wait(barrier, len(greeted))

    def part_of(ref, owner_chip, owner_core):
        return ref.at[
            pl.ds(pl.multiple_of(owner_core * rows, rows), rows),
            pl.ds(pl.multiple_of(owner_chip * wide, wide), wide),
        ]

    own_held = held.at[pl.ds(pl.multiple_of(replica * rows, rows), rows), :]

    def send_part(to_chip, to_core):
        to = {"replica": to_chip * 2 + to_core}
        send(part_of(grad_ref, to_chip, to_core), own_held, held_send, held_recv, to).start()

    def send_at(distance):
        @pl.when(chip + distance < chips)
        def _():
            send_part(chip + distance, core)
            send_part(chip + distance, 1 - core)

        @pl.when(chip >= distance)
        def _():
            send_part(chip - distance, core)
            send_part(chip - distance, 1 - core)

    def tell_both(stage, through):
        tell(reached.at[stage], device(dz=through))
        tell(reached.at[stage], device(dz=-through))

    tell_both(0, 2)
    grad_copy.wait()
    send_part(chip, 1 - core)
    pltpu.make_async_copy(part_of(grad_ref, chip, core), own_held, held_recv).start()
    send_at(1)
    send_at(2)
    pl.semaphore_wait(reached.at[0], 2)
    tell_both(1, 3)
    send_at(3)
    send_at(4)
    pl.semaphore_wait(reached.at[1], 2)
    tell_both(2, 1)
    send_at(5)
    send_at(6)
    send_at(7)

    if rows_x > 2:
        tell(beside_sem, device(dx=1))
        pl.semaphore_wait(beside_sem, 1)
    for dy in steps(rows_y):
        tell(near_row if dy == 1 else next_row, device(dy=dy))
    for dy in steps(rows_y):
        pl.semaphore_wait(near_row if dy == 1 else next_row, 1)
    if rows_y > 2:
        tell(far_row, device(dy=1))
        pl.semaphore_wait(far_row, 1)
    pl.semaphore_wait(reached.at[2], 2)

    kept = [
        pltpu.make_async_copy(params_hbm, params_ref, copy_sem.at[0]),
        pltpu.make_async_copy(first_hbm, first_ref, copy_sem.at[1]),
        pltpu.make_async_copy(second_hbm, second_ref, copy_sem.at[2]),
    ]
    for copy in kept:
        copy.start()
    weight_copy.wait()

    await_bytes(held, held_recv)
    core_small[...] = packed_gram(held[...], groups, rows)

    exchange = send(core_small, core_slot, core_sem, core_sum_recv, device(other=True))
    exchange.start()
    exchange.wait()
    plane_small[...] = core_small[...] + core_slot[...]

    if plane > 1:
        pltpu.make_async_copy(plane_small, plane_slots.at[y * rows_x + x], plane_recv).start()
        for step in sorted(range(1, plane), key=lambda step: -hops(step % rows_x, rows_x) - hops(step // rows_x, rows_y)):
            to = device(dx=step % rows_x, dy=step // rows_x)
            send(plane_small, plane_slots.at[y * rows_x + x], plane_send, plane_recv, to).start()
        await_bytes(plane_slots, plane_recv)
        ring_small[...] = jnp.sum(plane_slots[...], axis=0)
    else:
        ring_small[...] = plane_small[...]

    pltpu.make_async_copy(ring_small, ring_slots.at[z], ring_recv).start()
    for step in sorted(range(1, ring), key=lambda step: -hops(step, ring)):
        send(ring_small, ring_slots.at[z], ring_send, ring_recv, device(dz=step)).start()
    await_bytes(ring_slots, ring_recv)
    weights = median_weights(jnp.sum(ring_slots[...], axis=0), weight_ref, groups, entries)

    total = jnp.zeros((rows, wide), jnp.float32)
    for group in range(groups):
        total += weights[group : group + 1, :1] * held[group * rows : (group + 1) * rows, :].astype(jnp.float32)
    part_of(out_ref, chip, core)[...] = total

    sibling = {"replica": chip * 2 + 1 - core}
    tree, pieces = GATHER
    cut = rows // pieces
    place = [chip]
    for offset in range(1, chips):
        top = 1 << (offset.bit_length() - 1)
        below = place[offset - top]
        place.append(below + top - 2 * top * lax.rem(lax.div(below, top), 2))

    def piece_of(offset, piece, from_core):
        return out_ref.at[
            pl.ds(pl.multiple_of(from_core * rows + piece * cut, cut), cut),
            pl.ds(pl.multiple_of(place[offset] * wide, wide), wide),
        ]

    def to_chip(child, piece):
        parent = tree[child]
        part = piece_of(parent, piece, core)
        to = {"replica": place[parent ^ child] * 2 + core}
        return send(part, part, chip_send.at[child, piece], chip_recv.at[child, piece], to)

    def from_chip(child, piece):
        part = piece_of(child, piece, core)
        return pltpu.make_async_copy(part, part, chip_recv.at[child, piece])

    def to_core(offset, piece, from_core):
        part = piece_of(offset, piece, from_core)
        return send(part, part, core_send.at[offset, piece], core_recv.at[offset, piece], sibling)

    for piece in range(pieces):
        for child in tree:
            if tree[child] == 0:
                to_chip(child, piece).start()
        to_core(0, piece, core).start()
    for depth in range(1, 4):
        for piece in range(pieces):
            for offset in tree:
                if depth_of(tree, offset) != depth:
                    continue
                from_chip(offset, piece).wait()
                for child in tree:
                    if tree[child] == offset:
                        to_chip(child, piece).start()
                to_core(offset, piece, core).start()
    for offset in range(chips):
        for piece in range(pieces):
            to_core(offset, piece, 1 - core).wait_recv()
    for offset in range(chips):
        for piece in range(pieces):
            to_core(offset, piece, core).wait_send()
            if offset > 0:
                to_chip(offset, piece).wait_send()
    for copy in kept:
        copy.wait()
    await_bytes(held.at[pl.ds(0, (groups - 1) * rows), :], held_send)
    if plane > 1:
        await_bytes(plane_slots.at[pl.ds(0, plane - 1)], plane_send)
    await_bytes(ring_slots.at[pl.ds(0, ring - 1)], ring_send)


def update_kernel(
    median_ref, params_ref, first_ref, second_ref, median_hbm, params_hbm, first_hbm, second_hbm,
    params_new, first_new, second_new, median_sem, sems,
):
    median_copy = pltpu.make_async_copy(median_ref, median_hbm, median_sem)
    median_copy.start()
    rows, width = median_ref.shape
    cut = 8
    copies = []
    for part in range(rows // cut):
        at = pl.ds(part * cut, cut)
        median = median_ref[at, :]
        new_first = beta_first * first_ref[at, :] + (1.0 - beta_first) * median
        new_second = beta_second * second_ref[at, :] + (1.0 - beta_second) * median * median
        first_hat = new_first / (1.0 - beta_first**STEP)
        second_hat = new_second / (1.0 - beta_second**STEP)
        params = params_ref[at, :]
        params_new[at, :] = params - learn_rate * (
            first_hat / (jnp.sqrt(second_hat) + adam_epsilon) + decay_rate * params
        )
        first_new[at, :] = new_first
        second_new[at, :] = new_second
        for kind, (new, hbm) in enumerate(
            ((params_new, params_hbm), (first_new, first_hbm), (second_new, second_hbm))
        ):
            copy = pltpu.make_async_copy(new.at[at, :], hbm.at[at, :], sems.at[part, kind])
            copy.start()
            copies.append(copy)
    for copy in copies:
        copy.wait()
    median_copy.wait()


def body(chips, grid, gradients, replica_weight, params, first_moment, second_moment):
    rows_here, width = gradients.shape[1], gradients.shape[2]
    rows_y, runs, rows_x = grid
    groups, ring = 2 * chips, runs * chips
    entries = rows_here * rows_y * runs * rows_x * width
    rows, wide = rows_here // 2, width // chips
    dma, regular = pltpu.SemaphoreType.DMA, pltpu.SemaphoreType.REGULAR
    whole = jax.ShapeDtypeStruct((rows_here, width), jnp.float32)
    in_hbm = pl.BlockSpec(memory_space=pltpu.HBM)
    in_vmem = pl.BlockSpec(memory_space=pltpu.VMEM)
    small = pltpu.VMEM((2, LANES), jnp.float32)
    inputs = (gradients.reshape(rows_here, width), replica_weight, params, first_moment, second_moment)
    gathered = pl.pallas_call(
        functools.partial(kernel, chips, grid, entries),
        out_shape=(whole,) * 4,
        in_specs=[in_hbm] * 5,
        out_specs=(in_vmem,) * 4,
        scratch_shapes=[
            pltpu.VMEM((rows_here, width), jnp.bfloat16),
            pltpu.SMEM((groups,), jnp.float32),
            pltpu.VMEM((groups * rows, wide), jnp.bfloat16),
            small, small, small, small,
            pltpu.VMEM((rows_x * rows_y, 2, LANES), jnp.float32),
            pltpu.VMEM((ring, 2, LANES), jnp.float32),
            regular((3,)), regular, regular, regular, regular,
            dma, dma, dma((3,)), dma, dma, dma, dma,
            dma, dma, dma, dma,
            dma((chips, PIECES)), dma((chips, PIECES)), dma((chips, PIECES)), dma((chips, PIECES)),
        ],
        compiler_params=pltpu.CompilerParams(collective_id=0, has_side_effects=True, vmem_limit_bytes=51 * 1024 * 1024),
        name="median_rows",
    )(*(pltpu.with_memory_space_constraint(array, pltpu.HBM) for array in inputs))
    kept = pltpu.VMEM((rows_here, width), jnp.float32)
    return pl.pallas_call(
        update_kernel,
        out_shape=(whole,) * 4,
        in_specs=[in_vmem] * 4,
        out_specs=(in_hbm,) * 4,
        scratch_shapes=[kept, kept, kept, dma, dma((rows_here // 8, 3))],
        compiler_params=pltpu.CompilerParams(vmem_limit_bytes=16 * 1024 * 1024),
        name="update",
    )(*gathered)


def solution(mesh):
    chips = mesh.shape["replica"] // 2
    side = math.isqrt(mesh.shape["fsdp"] // 2)
    return jax.shard_map(
        functools.partial(body, chips, (side, 2, side)),
        mesh=mesh,
        in_specs=(
            P("replica", "fsdp", None),
            P(),
            P("fsdp", None),
            P("fsdp", None),
            P("fsdp", None),
        ),
        out_specs=(P("fsdp", None), P("fsdp", None), P("fsdp", None), P("fsdp", None)),
        check_vma=False,
    )
```

```python
import functools
import math

import jax
import jax.numpy as jnp
from jax import lax
from jax.experimental import pallas as pl
from jax.experimental.pallas import tpu as pltpu
from jax.sharding import PartitionSpec as P

ITERS = 4
STEP = 100

smooth_floor = 0.05
beta_first = 0.9
beta_second = 0.95
learn_rate = 0.001
decay_rate = 0.1
adam_epsilon = 1e-08

MESH = pl.DeviceIdType.MESH
LANES = 128
SPREAD = {4: 0, 2: 0, 1: 0, 3: 0, 6: 4, 5: 4, 7: 4}
SPREAD_TWICE = {1: 0, 2: 0, 3: 0, 5: 4, 6: 4, 7: 4}
TWICE_LANES = 384
MIRROR_AT = 1


def depth_of(tree, offset):
    return 0 if offset not in tree else 1 + depth_of(tree, tree[offset])


def packed_gram(block, groups, rows):
    product = lax.dot_general(block, block, (((1,), (1,)), ((), ())), preferred_element_type=jnp.float32)
    size = groups * rows
    row = lax.broadcasted_iota(jnp.int32, (size, size), 0)
    column = lax.broadcasted_iota(jnp.int32, (size, size), 1)
    same = lax.rem(row, rows) == lax.rem(column, rows)
    by_group = jnp.sum(jnp.where(same, product, 0.0).reshape(groups, rows, size), axis=1)
    lane = lax.broadcasted_iota(jnp.int32, (groups, LANES), 1)

    def fold(low, high, step):
        low, high = low + pltpu.roll(low, LANES - step, 1), high + pltpu.roll(high, step, 1)
        return jnp.where(lax.rem(lane[: low.shape[0]], 2 * step) < step, low, high)

    folded = fold(by_group[:, :LANES], by_group[:, LANES:], 8)
    folded = fold(folded[:8], folded[8:], 4)
    folded = fold(folded[:4], folded[4:], 2)
    return fold(folded[:2], folded[2:], 1)


def median_weights(packed, weight_ref, groups, entries):
    lane = lax.broadcasted_iota(jnp.int32, (groups, LANES), 1)
    sub = lax.broadcasted_iota(jnp.int32, (groups, LANES), 0)
    lane_group = lax.div(lane, 16) + 8 * lax.div(lax.rem(lane, 16), 8)
    here = lax.rem(lane, 8) == lax.div(sub, 2)
    both = jnp.where(lax.rem(sub, 2) == 0, packed[:1], packed[1:])
    gram = jnp.where(here, both, 0.0) * (1.0 / entries)
    own_lane = lane_group == sub
    given = jnp.zeros((groups, LANES), jnp.float32)
    for group in range(groups):
        given = jnp.where(sub == group, weight_ref[group], given)
    norm = jnp.sum(jnp.where(own_lane, gram, 0.0), axis=1, keepdims=True)
    weight = given
    for iteration in range(ITERS + 1):
        weight = weight / jnp.sum(weight, axis=0, keepdims=True)
        if iteration == ITERS:
            break
        along_lanes = jnp.sum(jnp.where(own_lane, weight, 0.0), axis=0, keepdims=True)
        product = jnp.sum(gram * along_lanes, axis=1, keepdims=True)
        squared = norm - 2.0 * product + jnp.sum(weight * product, axis=0, keepdims=True)
        weight = given / jnp.maximum(jnp.sqrt(jnp.maximum(squared, 0.0)), smooth_floor)
    return weight


def kernel(
    chips, grid, entries, grad_hbm, weight_hbm, params_hbm, first_hbm, second_hbm,
    out_ref, params_ref, first_ref, second_ref,
    grad_ref, weight_ref, held, held_twice, core_small, plane_small, ring_small, core_slot, plane_slots, ring_slots,
    reached, beside_sem, near_row, next_row, far_row,
    grad_sem, weight_sem, copy_sem, held_send, held_recv, twice_send, twice_recv, core_sem, core_sum_recv,
    plane_send, plane_recv, ring_send, ring_recv,
    chip_send, chip_recv, core_send, core_recv,
):
    rows_y, runs, rows_x = grid
    groups, plane, ring = 2 * chips, rows_x * rows_y, runs * chips
    replica, fsdp = lax.axis_index("replica"), lax.axis_index("fsdp")
    chip, core = lax.div(replica, 2), lax.rem(replica, 2)
    x, run, y = lax.rem(fsdp, rows_x), lax.rem(lax.div(fsdp, rows_x), runs), lax.div(fsdp, rows_x * runs)
    z = run * chips + chip
    rows = grad_ref.shape[0] // 2
    wide = grad_ref.shape[1] // chips
    twice = held_twice.shape[1]

    def device(dz=0, dy=0, dx=0, other=False):
        to_z = lax.rem(z + dz + ring, ring)
        to_y = lax.rem(y + dy + rows_y, rows_y)
        to_x = lax.rem(x + dx + rows_x, rows_x)
        return {
            "replica": lax.rem(to_z, chips) * 2 + (1 - core if other else core),
            "fsdp": (to_y * runs + lax.div(to_z, chips)) * rows_x + to_x,
        }

    def hops(step, size):
        return min(step, size - step)

    def steps(size):
        return {1: (), 2: (1,)}.get(size, (1, -1))

    def tell(sem, to):
        pl.semaphore_signal(sem, inc=1, device_id=to, device_id_type=MESH)

    def send(src, dst, send_sem, recv_sem, to):
        return pltpu.make_async_remote_copy(
            src_ref=src, dst_ref=dst, send_sem=send_sem, recv_sem=recv_sem, device_id=to, device_id_type=MESH
        )

    def await_bytes(ref, sem):
        pltpu.make_async_copy(ref, ref, sem).wait()

    grad_copy = pltpu.make_async_copy(grad_hbm, grad_ref, grad_sem)
    grad_copy.start()
    weight_copy = pltpu.make_async_copy(weight_hbm, weight_ref, weight_sem)
    weight_copy.start()

    barrier = pltpu.get_barrier_semaphore()
    greeted = [device(dz=dz, other=other) for dz in (-2, -1, 1, 2) for other in (False, True)]
    greeted += [device(dy=dy) for dy in steps(rows_y)] + [device(dx=dx) for dx in steps(rows_x)]
    greeted += [device(other=True)]
    for to in greeted:
        tell(barrier, to)
    pl.semaphore_wait(barrier, len(greeted))

    def part_of(ref, owner_chip, owner_core):
        return ref.at[
            pl.ds(pl.multiple_of(owner_core * rows, rows), rows),
            pl.ds(pl.multiple_of(owner_chip * wide, wide), wide),
        ]

    own_held = held.at[pl.ds(pl.multiple_of(replica * rows, rows), rows), :]

    def send_part(to_chip, to_core):
        to = {"replica": to_chip * 2 + to_core}
        send(part_of(grad_ref, to_chip, to_core), own_held, held_send, held_recv, to).start()

    def send_at(distance):
        @pl.when(chip + distance < chips)
        def _():
            send_part(chip + distance, core)
            send_part(chip + distance, 1 - core)

        @pl.when(chip >= distance)
        def _():
            send_part(chip - distance, core)
            send_part(chip - distance, 1 - core)

    def tell_both(stage, through):
        tell(reached.at[stage], device(dz=through))
        tell(reached.at[stage], device(dz=-through))

    tell_both(0, 2)
    grad_copy.wait()
    send_part(chip, 1 - core)
    pltpu.make_async_copy(part_of(grad_ref, chip, core), own_held, held_recv).start()
    send_at(1)
    send_at(2)
    pl.semaphore_wait(reached.at[0], 2)
    tell_both(1, 3)
    send_at(3)
    send_at(4)
    pl.semaphore_wait(reached.at[1], 2)
    tell_both(2, 1)
    send_at(5)
    send_at(6)
    send_at(7)

    if rows_x > 2:
        tell(beside_sem, device(dx=1))
        pl.semaphore_wait(beside_sem, 1)
    for dy in steps(rows_y):
        tell(near_row if dy == 1 else next_row, device(dy=dy))
    for dy in steps(rows_y):
        pl.semaphore_wait(near_row if dy == 1 else next_row, 1)
    if rows_y > 2:
        tell(far_row, device(dy=1))
        pl.semaphore_wait(far_row, 1)
    pl.semaphore_wait(reached.at[2], 2)

    kept = [
        pltpu.make_async_copy(params_hbm, params_ref, copy_sem.at[0]),
        pltpu.make_async_copy(first_hbm, first_ref, copy_sem.at[1]),
        pltpu.make_async_copy(second_hbm, second_ref, copy_sem.at[2]),
    ]
    for copy in kept:
        copy.start()
    weight_copy.wait()

    across = chip + 4 - 8 * lax.div(chip, 4)
    own_twice = held_twice.at[pl.ds(pl.multiple_of(replica * rows, rows), rows), :]

    def twice_of(ref, owner_chip, owner_core):
        return ref.at[
            pl.ds(pl.multiple_of(owner_core * rows, rows), rows),
            pl.ds(pl.multiple_of(owner_chip * wide, wide), twice),
        ]

    def send_twice(step):
        to = lax.rem(replica + step, groups)
        to_chip = lax.div(to, 2)
        src = twice_of(grad_ref, to_chip + 4 - 8 * lax.div(to_chip, 4), lax.rem(to, 2))
        send(src, own_twice, twice_send, twice_recv, {"replica": to}).start()

    pltpu.make_async_copy(twice_of(grad_ref, across, core), own_twice, twice_recv).start()
    if MIRROR_AT == 0:
        for step in range(1, groups):
            send_twice(step)

    await_bytes(held, held_recv)
    core_small[...] = packed_gram(held[...], groups, rows)

    exchange = send(core_small, core_slot, core_sem, core_sum_recv, device(other=True))
    exchange.start()
    exchange.wait()
    plane_small[...] = core_small[...] + core_slot[...]

    if plane > 1:
        pltpu.make_async_copy(plane_small, plane_slots.at[y * rows_x + x], plane_recv).start()
        for step in sorted(range(1, plane), key=lambda step: -hops(step % rows_x, rows_x) - hops(step // rows_x, rows_y)):
            to = device(dx=step % rows_x, dy=step // rows_x)
            send(plane_small, plane_slots.at[y * rows_x + x], plane_send, plane_recv, to).start()
        if MIRROR_AT == 1:
            for step in range(1, groups):
                send_twice(step)
        await_bytes(plane_slots, plane_recv)
        ring_small[...] = jnp.sum(plane_slots[...], axis=0)
    else:
        ring_small[...] = plane_small[...]

    pltpu.make_async_copy(ring_small, ring_slots.at[z], ring_recv).start()
    for step in sorted(range(1, ring), key=lambda step: -hops(step, ring)):
        send(ring_small, ring_slots.at[z], ring_send, ring_recv, device(dz=step)).start()
    await_bytes(ring_slots, ring_recv)
    weights = median_weights(jnp.sum(ring_slots[...], axis=0), weight_ref, groups, entries)

    def pooled(block, width):
        total = jnp.zeros((rows, width), jnp.float32)
        for group in range(groups):
            total += weights[group : group + 1, :1] * block[group * rows : (group + 1) * rows, :].astype(jnp.float32)
        return total

    part_of(out_ref, chip, core)[...] = pooled(held, wide)
    await_bytes(held_twice, twice_recv)
    twice_of(out_ref, across, core)[...] = pooled(held_twice, twice)

    sibling = {"replica": chip * 2 + 1 - core}
    pieces = ((twice, wide - twice, SPREAD), (0, twice, SPREAD_TWICE))
    pieces = tuple(piece for piece in pieces if piece[1] > 0)
    place = [chip]
    for offset in range(1, chips):
        top = 1 << (offset.bit_length() - 1)
        below = place[offset - top]
        place.append(below + top - 2 * top * lax.rem(lax.div(below, top), 2))

    def piece_of(offset, piece, from_core):
        start, width, _ = pieces[piece]
        return out_ref.at[
            pl.ds(pl.multiple_of(from_core * rows, rows), rows),
            pl.ds(pl.multiple_of(place[offset] * wide + start, LANES), width),
        ]

    def to_chip(child, piece):
        parent = pieces[piece][2][child]
        part = piece_of(parent, piece, core)
        to = {"replica": place[parent ^ child] * 2 + core}
        return send(part, part, chip_send.at[child, piece], chip_recv.at[child, piece], to)

    def from_chip(child, piece):
        part = piece_of(child, piece, core)
        return pltpu.make_async_copy(part, part, chip_recv.at[child, piece])

    def to_core(offset, piece, from_core):
        part = piece_of(offset, piece, from_core)
        return send(part, part, core_send.at[offset, piece], core_recv.at[offset, piece], sibling)

    def passed_on(offset, piece):
        for child, parent in pieces[piece][2].items():
            if parent == offset:
                to_chip(child, piece).start()

    for piece, (_, _, tree) in enumerate(pieces):
        for offset in range(chips):
            if offset not in tree:
                passed_on(offset, piece)
    for piece, (_, _, tree) in enumerate(pieces):
        for offset in range(chips):
            if offset not in tree:
                to_core(offset, piece, core).start()
    for depth in (1, 2):
        for piece, (_, _, tree) in enumerate(pieces):
            for offset in tree:
                if depth_of(tree, offset) == depth:
                    from_chip(offset, piece).wait()
                    passed_on(offset, piece)
                    to_core(offset, piece, core).start()
    for piece, (_, _, tree) in enumerate(pieces):
        for offset in range(chips):
            to_core(offset, piece, 1 - core).wait_recv()
    for piece, (_, _, tree) in enumerate(pieces):
        for offset in range(chips):
            to_core(offset, piece, core).wait_send()
            if offset in tree:
                to_chip(offset, piece).wait_send()
    await_bytes(held_twice.at[pl.ds(0, (groups - 1) * rows), :], twice_send)
    for copy in kept:
        copy.wait()
    await_bytes(held.at[pl.ds(0, (groups - 1) * rows), :], held_send)
    if plane > 1:
        await_bytes(plane_slots.at[pl.ds(0, plane - 1)], plane_send)
    await_bytes(ring_slots.at[pl.ds(0, ring - 1)], ring_send)


def update_kernel(
    median_ref, params_ref, first_ref, second_ref, median_hbm, params_hbm, first_hbm, second_hbm,
    params_new, first_new, second_new, median_sem, sems,
):
    median_copy = pltpu.make_async_copy(median_ref, median_hbm, median_sem)
    median_copy.start()
    rows, width = median_ref.shape
    cut = 8
    copies = []
    for part in range(rows // cut):
        at = pl.ds(part * cut, cut)
        median = median_ref[at, :]
        new_first = beta_first * first_ref[at, :] + (1.0 - beta_first) * median
        new_second = beta_second * second_ref[at, :] + (1.0 - beta_second) * median * median
        first_hat = new_first / (1.0 - beta_first**STEP)
        second_hat = new_second / (1.0 - beta_second**STEP)
        params = params_ref[at, :]
        params_new[at, :] = params - learn_rate * (
            first_hat / (jnp.sqrt(second_hat) + adam_epsilon) + decay_rate * params
        )
        first_new[at, :] = new_first
        second_new[at, :] = new_second
        for kind, (new, hbm) in enumerate(
            ((params_new, params_hbm), (first_new, first_hbm), (second_new, second_hbm))
        ):
            copy = pltpu.make_async_copy(new.at[at, :], hbm.at[at, :], sems.at[part, kind])
            copy.start()
            copies.append(copy)
    for copy in copies:
        copy.wait()
    median_copy.wait()


def body(chips, grid, gradients, replica_weight, params, first_moment, second_moment):
    rows_here, width = gradients.shape[1], gradients.shape[2]
    rows_y, runs, rows_x = grid
    groups, ring = 2 * chips, runs * chips
    entries = rows_here * rows_y * runs * rows_x * width
    rows, wide = rows_here // 2, width // chips
    dma, regular = pltpu.SemaphoreType.DMA, pltpu.SemaphoreType.REGULAR
    whole = jax.ShapeDtypeStruct((rows_here, width), jnp.float32)
    in_hbm = pl.BlockSpec(memory_space=pltpu.HBM)
    in_vmem = pl.BlockSpec(memory_space=pltpu.VMEM)
    small = pltpu.VMEM((2, LANES), jnp.float32)
    inputs = (gradients.reshape(rows_here, width), replica_weight, params, first_moment, second_moment)
    gathered = pl.pallas_call(
        functools.partial(kernel, chips, grid, entries),
        out_shape=(whole,) * 4,
        in_specs=[in_hbm] * 5,
        out_specs=(in_vmem,) * 4,
        scratch_shapes=[
            pltpu.VMEM((rows_here, width), jnp.bfloat16),
            pltpu.SMEM((groups,), jnp.float32),
            pltpu.VMEM((groups * rows, wide), jnp.bfloat16),
            pltpu.VMEM((groups * rows, TWICE_LANES), jnp.bfloat16),
            small, small, small, small,
            pltpu.VMEM((rows_x * rows_y, 2, LANES), jnp.float32),
            pltpu.VMEM((ring, 2, LANES), jnp.float32),
            regular((3,)), regular, regular, regular, regular,
            dma, dma, dma((3,)), dma, dma, dma, dma, dma, dma,
            dma, dma, dma, dma,
            dma((chips, 2)), dma((chips, 2)), dma((chips, 2)), dma((chips, 2)),
        ],
        compiler_params=pltpu.CompilerParams(collective_id=0, has_side_effects=True, vmem_limit_bytes=51 * 1024 * 1024),
        name="median_rows",
    )(*(pltpu.with_memory_space_constraint(array, pltpu.HBM) for array in inputs))
    kept = pltpu.VMEM((rows_here, width), jnp.float32)
    return pl.pallas_call(
        update_kernel,
        out_shape=(whole,) * 4,
        in_specs=[in_vmem] * 4,
        out_specs=(in_hbm,) * 4,
        scratch_shapes=[kept, kept, kept, dma, dma((rows_here // 8, 3))],
        compiler_params=pltpu.CompilerParams(vmem_limit_bytes=16 * 1024 * 1024),
        name="update",
    )(*gathered)


def solution(mesh):
    chips = mesh.shape["replica"] // 2
    side = math.isqrt(mesh.shape["fsdp"] // 2)
    return jax.shard_map(
        functools.partial(body, chips, (side, 2, side)),
        mesh=mesh,
        in_specs=(
            P("replica", "fsdp", None),
            P(),
            P("fsdp", None),
            P("fsdp", None),
            P("fsdp", None),
        ),
        out_specs=(P("fsdp", None), P("fsdp", None), P("fsdp", None), P("fsdp", None)),
        check_vma=False,
    )
```

```python
import functools
import math

import jax
import jax.numpy as jnp
from jax import lax
from jax.experimental import pallas as pl
from jax.experimental.pallas import tpu as pltpu
from jax.sharding import PartitionSpec as P

ITERS = 4
STEP = 100

smooth_floor = 0.05
beta_first = 0.9
beta_second = 0.95
learn_rate = 0.001
decay_rate = 0.1
adam_epsilon = 1e-08

MESH = pl.DeviceIdType.MESH
LANES = 128
SPREAD = {4: 0, 2: 0, 1: 0, 3: 0, 6: 4, 5: 4, 7: 4}
SPREAD_TWICE = {1: 0, 2: 0, 3: 0, 5: 4, 6: 4, 7: 4}
TWICE_LANES = 384
ARRIVALS = [(0, 4), (0, 2), (0, 1), (0, 3), (1, 1), (1, 2), (1, 3), (1, 5), (1, 6), (1, 7), (0, 6), (0, 5), (0, 7)]


def packed_gram(block, groups, rows):
    product = lax.dot_general(block, block, (((1,), (1,)), ((), ())), preferred_element_type=jnp.float32)
    size = groups * rows
    row = lax.broadcasted_iota(jnp.int32, (size, size), 0)
    column = lax.broadcasted_iota(jnp.int32, (size, size), 1)
    same = lax.rem(row, rows) == lax.rem(column, rows)
    by_group = jnp.sum(jnp.where(same, product, 0.0).reshape(groups, rows, size), axis=1)
    lane = lax.broadcasted_iota(jnp.int32, (groups, LANES), 1)

    def fold(low, high, step):
        low, high = low + pltpu.roll(low, LANES - step, 1), high + pltpu.roll(high, step, 1)
        return jnp.where(lax.rem(lane[: low.shape[0]], 2 * step) < step, low, high)

    folded = fold(by_group[:, :LANES], by_group[:, LANES:], 8)
    folded = fold(folded[:8], folded[8:], 4)
    folded = fold(folded[:4], folded[4:], 2)
    return fold(folded[:2], folded[2:], 1)


def median_weights(packed, weight_ref, groups, entries):
    lane = lax.broadcasted_iota(jnp.int32, (groups, LANES), 1)
    sub = lax.broadcasted_iota(jnp.int32, (groups, LANES), 0)
    lane_group = lax.div(lane, 16) + 8 * lax.div(lax.rem(lane, 16), 8)
    here = lax.rem(lane, 8) == lax.div(sub, 2)
    both = jnp.where(lax.rem(sub, 2) == 0, packed[:1], packed[1:])
    gram = jnp.where(here, both, 0.0) * (1.0 / entries)
    own_lane = lane_group == sub
    given = jnp.zeros((groups, LANES), jnp.float32)
    for group in range(groups):
        given = jnp.where(sub == group, weight_ref[group], given)
    norm = jnp.sum(jnp.where(own_lane, gram, 0.0), axis=1, keepdims=True)
    weight = given
    for iteration in range(ITERS + 1):
        weight = weight / jnp.sum(weight, axis=0, keepdims=True)
        if iteration == ITERS:
            break
        along_lanes = jnp.sum(jnp.where(own_lane, weight, 0.0), axis=0, keepdims=True)
        product = jnp.sum(gram * along_lanes, axis=1, keepdims=True)
        squared = norm - 2.0 * product + jnp.sum(weight * product, axis=0, keepdims=True)
        weight = given / jnp.maximum(jnp.sqrt(jnp.maximum(squared, 0.0)), smooth_floor)
    return weight


def kernel(
    chips, grid, entries, grad_hbm, weight_hbm, params_hbm, first_hbm, second_hbm,
    out_ref, params_ref, first_ref, second_ref,
    grad_ref, weight_ref, held, held_twice, plane_small, ring_small, plane_slots, ring_slots,
    reached, both_sem, beside_sem, near_row, next_row, far_row,
    grad_sem, weight_sem, copy_sem, held_send, held_recv, twice_send, twice_recv,
    plane_send, plane_recv, ring_send, ring_recv,
    chip_send, chip_recv, core_send, core_recv,
):
    rows_y, runs, rows_x = grid
    groups, plane, ring = 2 * chips, rows_x * rows_y, runs * chips
    replica, fsdp = lax.axis_index("replica"), lax.axis_index("fsdp")
    chip, core = lax.div(replica, 2), lax.rem(replica, 2)
    x, run, y = lax.rem(fsdp, rows_x), lax.rem(lax.div(fsdp, rows_x), runs), lax.div(fsdp, rows_x * runs)
    z = run * chips + chip
    rows = grad_ref.shape[0] // 2
    wide = grad_ref.shape[1] // chips
    twice = held_twice.shape[1]

    def device(dz=0, dy=0, dx=0, other=False):
        to_z = lax.rem(z + dz + ring, ring)
        to_y = lax.rem(y + dy + rows_y, rows_y)
        to_x = lax.rem(x + dx + rows_x, rows_x)
        return {
            "replica": lax.rem(to_z, chips) * 2 + (1 - core if other else core),
            "fsdp": (to_y * runs + lax.div(to_z, chips)) * rows_x + to_x,
        }

    def hops(step, size):
        return min(step, size - step)

    def steps(size):
        return {1: (), 2: (1,)}.get(size, (1, -1))

    def tell(sem, to):
        pl.semaphore_signal(sem, inc=1, device_id=to, device_id_type=MESH)

    def send(src, dst, send_sem, recv_sem, to):
        return pltpu.make_async_remote_copy(
            src_ref=src, dst_ref=dst, send_sem=send_sem, recv_sem=recv_sem, device_id=to, device_id_type=MESH
        )

    def await_bytes(ref, sem):
        pltpu.make_async_copy(ref, ref, sem).wait()

    grad_copy = pltpu.make_async_copy(grad_hbm, grad_ref, grad_sem)
    grad_copy.start()
    weight_copy = pltpu.make_async_copy(weight_hbm, weight_ref, weight_sem)
    weight_copy.start()

    barrier = pltpu.get_barrier_semaphore()
    greeted = [device(dz=dz, other=other) for dz in (-2, -1, 1, 2) for other in (False, True)]
    greeted += [device(dy=dy) for dy in steps(rows_y)] + [device(dx=dx) for dx in steps(rows_x)]
    greeted += [device(other=True)]
    for to in greeted:
        tell(barrier, to)
    pl.semaphore_wait(barrier, len(greeted))

    def part_of(ref, owner_chip, owner_core):
        return ref.at[
            pl.ds(pl.multiple_of(owner_core * rows, rows), rows),
            pl.ds(pl.multiple_of(owner_chip * wide, wide), wide),
        ]

    own_held = held.at[pl.ds(pl.multiple_of(replica * rows, rows), rows), :]

    def send_part(to_chip, to_core):
        to = {"replica": to_chip * 2 + to_core}
        send(part_of(grad_ref, to_chip, to_core), own_held, held_send, held_recv, to).start()

    def send_at(distance):
        @pl.when(chip + distance < chips)
        def _():
            send_part(chip + distance, core)
            send_part(chip + distance, 1 - core)

        @pl.when(chip >= distance)
        def _():
            send_part(chip - distance, core)
            send_part(chip - distance, 1 - core)

    def tell_both(stage, through):
        tell(reached.at[stage], device(dz=through))
        tell(reached.at[stage], device(dz=-through))

    tell_both(0, 2)
    grad_copy.wait()
    send_part(chip, 1 - core)
    pltpu.make_async_copy(part_of(grad_ref, chip, core), own_held, held_recv).start()
    send_at(1)
    send_at(2)
    pl.semaphore_wait(reached.at[0], 2)
    tell_both(1, 3)
    send_at(3)
    send_at(4)
    pl.semaphore_wait(reached.at[1], 2)
    tell_both(2, 1)
    send_at(5)
    send_at(6)
    send_at(7)

    for dx in steps(rows_x):
        tell(both_sem, device(dx=dx))
    if rows_x > 1:
        pl.semaphore_wait(both_sem, len(steps(rows_x)))
    if rows_x > 2:
        tell(beside_sem, device(dx=1))
        pl.semaphore_wait(beside_sem, 1)
    for dy in steps(rows_y):
        tell(near_row if dy == 1 else next_row, device(dy=dy))
    for dy in steps(rows_y):
        pl.semaphore_wait(near_row if dy == 1 else next_row, 1)
    if rows_y > 2:
        tell(far_row, device(dy=1))
        pl.semaphore_wait(far_row, 1)
    pl.semaphore_wait(reached.at[2], 2)

    kept = [
        pltpu.make_async_copy(params_hbm, params_ref, copy_sem.at[0]),
        pltpu.make_async_copy(first_hbm, first_ref, copy_sem.at[1]),
        pltpu.make_async_copy(second_hbm, second_ref, copy_sem.at[2]),
    ]
    for copy in kept:
        copy.start()
    weight_copy.wait()

    across = chip + 4 - 8 * lax.div(chip, 4)
    own_twice = held_twice.at[pl.ds(pl.multiple_of(replica * rows, rows), rows), :]

    def twice_of(ref, owner_chip, owner_core):
        return ref.at[
            pl.ds(pl.multiple_of(owner_core * rows, rows), rows),
            pl.ds(pl.multiple_of(owner_chip * wide, wide), twice),
        ]

    def send_twice(step):
        to = lax.rem(replica + step, groups)
        to_chip = lax.div(to, 2)
        src = twice_of(grad_ref, to_chip + 4 - 8 * lax.div(to_chip, 4), lax.rem(to, 2))
        send(src, own_twice, twice_send, twice_recv, {"replica": to}).start()

    pltpu.make_async_copy(twice_of(grad_ref, across, core), own_twice, twice_recv).start()

    await_bytes(held, held_recv)
    plane_small[...] = packed_gram(held[...], groups, rows)

    own_slot = plane_slots.at[(y * rows_x + x) * 2 + core]
    pltpu.make_async_copy(plane_small, own_slot, plane_recv).start()
    far_first = sorted(range(plane), key=lambda step: -hops(step % rows_x, rows_x) - hops(step // rows_x, rows_y))
    for step in far_first:
        for other in (False, True):
            if step > 0 or other:
                to = device(dx=step % rows_x, dy=step // rows_x, other=other)
                send(plane_small, own_slot, plane_send, plane_recv, to).start()
    for step in range(1, groups):
        send_twice(step)
    await_bytes(plane_slots, plane_recv)
    ring_small[...] = jnp.sum(plane_slots[...], axis=0)

    pltpu.make_async_copy(ring_small, ring_slots.at[z], ring_recv).start()
    for step in sorted(range(1, ring), key=lambda step: -hops(step, ring)):
        send(ring_small, ring_slots.at[z], ring_send, ring_recv, device(dz=step)).start()
    await_bytes(ring_slots, ring_recv)
    weights = median_weights(jnp.sum(ring_slots[...], axis=0), weight_ref, groups, entries)

    def pooled(block, width):
        total = jnp.zeros((rows, width), jnp.float32)
        for group in range(groups):
            total += weights[group : group + 1, :1] * block[group * rows : (group + 1) * rows, :].astype(jnp.float32)
        return total

    part_of(out_ref, chip, core)[...] = pooled(held, wide)

    sibling = {"replica": chip * 2 + 1 - core}
    pieces = ((twice, wide - twice, SPREAD), (0, twice, SPREAD_TWICE))
    place = [chip]
    for offset in range(1, chips):
        top = 1 << (offset.bit_length() - 1)
        below = place[offset - top]
        place.append(below + top - 2 * top * lax.rem(lax.div(below, top), 2))

    def piece_of(offset, piece, from_core):
        start, width, _ = pieces[piece]
        return out_ref.at[
            pl.ds(pl.multiple_of(from_core * rows, rows), rows),
            pl.ds(pl.multiple_of(place[offset] * wide + start, LANES), width),
        ]

    def to_chip(child, piece):
        parent = pieces[piece][2][child]
        part = piece_of(parent, piece, core)
        to = {"replica": place[parent ^ child] * 2 + core}
        return send(part, part, chip_send.at[child, piece], chip_recv.at[child, piece], to)

    def from_chip(child, piece):
        part = piece_of(child, piece, core)
        return pltpu.make_async_copy(part, part, chip_recv.at[child, piece])

    def to_core(offset, piece, from_core):
        part = piece_of(offset, piece, from_core)
        return send(part, part, core_send.at[offset, piece], core_recv.at[offset, piece], sibling)

    def passed_on(offset, piece):
        for child, parent in pieces[piece][2].items():
            if parent == offset:
                to_chip(child, piece).start()

    for piece in range(2):
        passed_on(0, piece)
    for piece in range(2):
        to_core(0, piece, core).start()
    await_bytes(held_twice, twice_recv)
    twice_of(out_ref, across, core)[...] = pooled(held_twice, twice)
    passed_on(4, 1)
    to_core(4, 1, core).start()
    for piece, offset in ARRIVALS:
        from_chip(offset, piece).wait()
        passed_on(offset, piece)
        to_core(offset, piece, core).start()
    for piece, (_, _, tree) in enumerate(pieces):
        for offset in range(chips):
            to_core(offset, piece, 1 - core).wait_recv()
    for piece, (_, _, tree) in enumerate(pieces):
        for offset in range(chips):
            to_core(offset, piece, core).wait_send()
            if offset in tree:
                to_chip(offset, piece).wait_send()
    await_bytes(held_twice.at[pl.ds(0, (groups - 1) * rows), :], twice_send)
    for copy in kept:
        copy.wait()
    await_bytes(held.at[pl.ds(0, (groups - 1) * rows), :], held_send)
    await_bytes(plane_slots.at[pl.ds(0, 2 * plane - 1)], plane_send)
    await_bytes(ring_slots.at[pl.ds(0, ring - 1)], ring_send)


def update_kernel(
    median_ref, params_ref, first_ref, second_ref, median_hbm, params_hbm, first_hbm, second_hbm,
    params_new, first_new, second_new, median_sem, sems,
):
    median_copy = pltpu.make_async_copy(median_ref, median_hbm, median_sem)
    median_copy.start()
    rows, width = median_ref.shape
    cut = 8
    copies = []
    for part in range(rows // cut):
        at = pl.ds(part * cut, cut)
        median = median_ref[at, :]
        new_first = beta_first * first_ref[at, :] + (1.0 - beta_first) * median
        new_second = beta_second * second_ref[at, :] + (1.0 - beta_second) * median * median
        first_hat = new_first / (1.0 - beta_first**STEP)
        second_hat = new_second / (1.0 - beta_second**STEP)
        params = params_ref[at, :]
        params_new[at, :] = params - learn_rate * (
            first_hat / (jnp.sqrt(second_hat) + adam_epsilon) + decay_rate * params
        )
        first_new[at, :] = new_first
        second_new[at, :] = new_second
        for kind, (new, hbm) in enumerate(
            ((params_new, params_hbm), (first_new, first_hbm), (second_new, second_hbm))
        ):
            copy = pltpu.make_async_copy(new.at[at, :], hbm.at[at, :], sems.at[part, kind])
            copy.start()
            copies.append(copy)
    for copy in copies:
        copy.wait()
    median_copy.wait()


def body(chips, grid, gradients, replica_weight, params, first_moment, second_moment):
    rows_here, width = gradients.shape[1], gradients.shape[2]
    rows_y, runs, rows_x = grid
    groups, ring = 2 * chips, runs * chips
    entries = rows_here * rows_y * runs * rows_x * width
    rows, wide = rows_here // 2, width // chips
    dma, regular = pltpu.SemaphoreType.DMA, pltpu.SemaphoreType.REGULAR
    whole = jax.ShapeDtypeStruct((rows_here, width), jnp.float32)
    in_hbm = pl.BlockSpec(memory_space=pltpu.HBM)
    in_vmem = pl.BlockSpec(memory_space=pltpu.VMEM)
    small = pltpu.VMEM((2, LANES), jnp.float32)
    inputs = (gradients.reshape(rows_here, width), replica_weight, params, first_moment, second_moment)
    gathered = pl.pallas_call(
        functools.partial(kernel, chips, grid, entries),
        out_shape=(whole,) * 4,
        in_specs=[in_hbm] * 5,
        out_specs=(in_vmem,) * 4,
        scratch_shapes=[
            pltpu.VMEM((rows_here, width), jnp.bfloat16),
            pltpu.SMEM((groups,), jnp.float32),
            pltpu.VMEM((groups * rows, wide), jnp.bfloat16),
            pltpu.VMEM((groups * rows, TWICE_LANES), jnp.bfloat16),
            small, small,
            pltpu.VMEM((2 * rows_x * rows_y, 2, LANES), jnp.float32),
            pltpu.VMEM((ring, 2, LANES), jnp.float32),
            regular((3,)), regular, regular, regular, regular, regular,
            dma, dma, dma((3,)), dma, dma, dma, dma,
            dma, dma, dma, dma,
            dma((chips, 2)), dma((chips, 2)), dma((chips, 2)), dma((chips, 2)),
        ],
        compiler_params=pltpu.CompilerParams(collective_id=0, has_side_effects=True, vmem_limit_bytes=51 * 1024 * 1024),
        name="median_rows",
    )(*(pltpu.with_memory_space_constraint(array, pltpu.HBM) for array in inputs))
    kept = pltpu.VMEM((rows_here, width), jnp.float32)
    return pl.pallas_call(
        update_kernel,
        out_shape=(whole,) * 4,
        in_specs=[in_vmem] * 4,
        out_specs=(in_hbm,) * 4,
        scratch_shapes=[kept, kept, kept, dma, dma((rows_here // 8, 3))],
        compiler_params=pltpu.CompilerParams(vmem_limit_bytes=16 * 1024 * 1024),
        name="update",
    )(*gathered)


def solution(mesh):
    chips = mesh.shape["replica"] // 2
    side = math.isqrt(mesh.shape["fsdp"] // 2)
    return jax.shard_map(
        functools.partial(body, chips, (side, 2, side)),
        mesh=mesh,
        in_specs=(
            P("replica", "fsdp", None),
            P(),
            P("fsdp", None),
            P("fsdp", None),
            P("fsdp", None),
        ),
        out_specs=(P("fsdp", None), P("fsdp", None), P("fsdp", None), P("fsdp", None)),
        check_vma=False,
    )
```

```python
import functools
import math

import jax
import jax.numpy as jnp
from jax import lax
from jax.experimental import pallas as pl
from jax.experimental.pallas import tpu as pltpu
from jax.sharding import PartitionSpec as P

ITERS = 4
STEP = 100

smooth_floor = 0.05
beta_first = 0.9
beta_second = 0.95
learn_rate = 0.001
decay_rate = 0.1
adam_epsilon = 1e-08

MESH = pl.DeviceIdType.MESH
LANES = 128
SPREAD = {4: 0, 2: 0, 1: 0, 3: 0, 6: 4, 5: 4, 7: 4}
SPREAD_TWICE = {1: 0, 2: 0, 3: 0, 5: 4, 6: 4, 7: 4}
TWICE_LANES = 384
ARRIVALS = [(0, 4), (0, 2), (0, 1), (0, 3), (1, 1), (1, 2), (1, 3), (1, 5), (1, 6), (1, 7), (0, 6), (0, 5), (0, 7)]


def packed_gram(block, groups, rows):
    product = lax.dot_general(block, block, (((1,), (1,)), ((), ())), preferred_element_type=jnp.float32)
    size = groups * rows
    row = lax.broadcasted_iota(jnp.int32, (size, size), 0)
    column = lax.broadcasted_iota(jnp.int32, (size, size), 1)
    same = lax.rem(row, rows) == lax.rem(column, rows)
    by_group = jnp.sum(jnp.where(same, product, 0.0).reshape(groups, rows, size), axis=1)
    lane = lax.broadcasted_iota(jnp.int32, (groups, LANES), 1)

    def fold(low, high, step):
        low, high = low + pltpu.roll(low, LANES - step, 1), high + pltpu.roll(high, step, 1)
        return jnp.where(lax.rem(lane[: low.shape[0]], 2 * step) < step, low, high)

    folded = fold(by_group[:, :LANES], by_group[:, LANES:], 8)
    folded = fold(folded[:8], folded[8:], 4)
    folded = fold(folded[:4], folded[4:], 2)
    return fold(folded[:2], folded[2:], 1)


def median_weights(packed, weight_ref, groups, entries):
    lane = lax.broadcasted_iota(jnp.int32, (groups, LANES), 1)
    sub = lax.broadcasted_iota(jnp.int32, (groups, LANES), 0)
    lane_group = lax.div(lane, 16) + 8 * lax.div(lax.rem(lane, 16), 8)
    here = lax.rem(lane, 8) == lax.div(sub, 2)
    both = jnp.where(lax.rem(sub, 2) == 0, packed[:1], packed[1:])
    gram = jnp.where(here, both, 0.0) * (1.0 / entries)
    own_lane = lane_group == sub
    given = jnp.zeros((groups, LANES), jnp.float32)
    for group in range(groups):
        given = jnp.where(sub == group, weight_ref[group], given)
    norm = jnp.sum(jnp.where(own_lane, gram, 0.0), axis=1, keepdims=True)
    weight = given
    for iteration in range(ITERS + 1):
        weight = weight / jnp.sum(weight, axis=0, keepdims=True)
        if iteration == ITERS:
            break
        along_lanes = jnp.sum(jnp.where(own_lane, weight, 0.0), axis=0, keepdims=True)
        product = jnp.sum(gram * along_lanes, axis=1, keepdims=True)
        squared = norm - 2.0 * product + jnp.sum(weight * product, axis=0, keepdims=True)
        weight = given / jnp.maximum(jnp.sqrt(jnp.maximum(squared, 0.0)), smooth_floor)
    return weight


def kernel(
    chips, grid, entries, grad_hbm, weight_hbm, params_hbm, first_hbm, second_hbm,
    out_ref, params_ref, first_ref, second_ref,
    grad_ref, weight_ref, held, held_twice, plane_small, ring_small, plane_slots, ring_slots,
    reached, both_sem, beside_sem, near_row, next_row, far_row,
    grad_sem, weight_sem, copy_sem, held_send, held_recv, twice_send, twice_recv,
    plane_send, plane_recv, ring_send, ring_recv,
    chip_send, chip_recv, core_send, core_recv,
):
    rows_y, runs, rows_x = grid
    groups, plane, ring = 2 * chips, rows_x * rows_y, runs * chips
    replica, fsdp = lax.axis_index("replica"), lax.axis_index("fsdp")
    chip, core = lax.div(replica, 2), lax.rem(replica, 2)
    x, run, y = lax.rem(fsdp, rows_x), lax.rem(lax.div(fsdp, rows_x), runs), lax.div(fsdp, rows_x * runs)
    z = run * chips + chip
    rows = grad_ref.shape[0] // 2
    wide = grad_ref.shape[1] // chips
    twice = held_twice.shape[1]

    def device(dz=0, dy=0, dx=0, other=False):
        to_z = lax.rem(z + dz + ring, ring)
        to_y = lax.rem(y + dy + rows_y, rows_y)
        to_x = lax.rem(x + dx + rows_x, rows_x)
        return {
            "replica": lax.rem(to_z, chips) * 2 + (1 - core if other else core),
            "fsdp": (to_y * runs + lax.div(to_z, chips)) * rows_x + to_x,
        }

    def hops(step, size):
        return min(step, size - step)

    def steps(size):
        return {1: (), 2: (1,)}.get(size, (1, -1))

    def tell(sem, to):
        pl.semaphore_signal(sem, inc=1, device_id=to, device_id_type=MESH)

    def send(src, dst, send_sem, recv_sem, to):
        return pltpu.make_async_remote_copy(
            src_ref=src, dst_ref=dst, send_sem=send_sem, recv_sem=recv_sem, device_id=to, device_id_type=MESH
        )

    def await_bytes(ref, sem):
        pltpu.make_async_copy(ref, ref, sem).wait()

    barrier = pltpu.get_barrier_semaphore()
    greeted = [device(dz=dz, other=other) for dz in (-2, -1, 1, 2) for other in (False, True)]
    greeted += [device(dy=dy) for dy in steps(rows_y)] + [device(dx=dx) for dx in steps(rows_x)]
    greeted += [device(other=True)]
    for to in greeted:
        tell(barrier, to)
    grad_copy = pltpu.make_async_copy(grad_hbm, grad_ref, grad_sem)
    grad_copy.start()
    weight_copy = pltpu.make_async_copy(weight_hbm, weight_ref, weight_sem)
    weight_copy.start()
    pl.semaphore_wait(barrier, len(greeted))

    def part_of(ref, owner_chip, owner_core):
        return ref.at[
            pl.ds(pl.multiple_of(owner_core * rows, rows), rows),
            pl.ds(pl.multiple_of(owner_chip * wide, wide), wide),
        ]

    own_held = held.at[pl.ds(pl.multiple_of(replica * rows, rows), rows), :]

    def send_part(to_chip, to_core):
        to = {"replica": to_chip * 2 + to_core}
        send(part_of(grad_ref, to_chip, to_core), own_held, held_send, held_recv, to).start()

    def send_at(distance):
        @pl.when(chip + distance < chips)
        def _():
            send_part(chip + distance, core)
            send_part(chip + distance, 1 - core)

        @pl.when(chip >= distance)
        def _():
            send_part(chip - distance, core)
            send_part(chip - distance, 1 - core)

    def tell_both(stage, through):
        tell(reached.at[stage], device(dz=through))
        tell(reached.at[stage], device(dz=-through))

    tell_both(0, 2)
    grad_copy.wait()
    send_part(chip, 1 - core)
    pltpu.make_async_copy(part_of(grad_ref, chip, core), own_held, held_recv).start()
    send_at(1)
    send_at(2)
    pl.semaphore_wait(reached.at[0], 2)
    tell_both(1, 3)
    send_at(3)
    send_at(4)
    pl.semaphore_wait(reached.at[1], 2)
    tell_both(2, 1)
    send_at(5)
    send_at(6)
    send_at(7)

    for dx in steps(rows_x):
        tell(both_sem, device(dx=dx))
    if rows_x > 1:
        pl.semaphore_wait(both_sem, len(steps(rows_x)))
    if rows_x > 2:
        tell(beside_sem, device(dx=1))
        pl.semaphore_wait(beside_sem, 1)
    for dy in steps(rows_y):
        tell(near_row if dy == 1 else next_row, device(dy=dy))
    for dy in steps(rows_y):
        pl.semaphore_wait(near_row if dy == 1 else next_row, 1)
    if rows_y > 2:
        tell(far_row, device(dy=1))
        pl.semaphore_wait(far_row, 1)
    pl.semaphore_wait(reached.at[2], 2)

    kept = [
        pltpu.make_async_copy(params_hbm, params_ref, copy_sem.at[0]),
        pltpu.make_async_copy(first_hbm, first_ref, copy_sem.at[1]),
        pltpu.make_async_copy(second_hbm, second_ref, copy_sem.at[2]),
    ]
    for copy in kept:
        copy.start()
    weight_copy.wait()

    across = chip + 4 - 8 * lax.div(chip, 4)
    own_twice = held_twice.at[pl.ds(pl.multiple_of(replica * rows, rows), rows), :]

    def twice_of(ref, owner_chip, owner_core):
        return ref.at[
            pl.ds(pl.multiple_of(owner_core * rows, rows), rows),
            pl.ds(pl.multiple_of(owner_chip * wide, wide), twice),
        ]

    def send_twice(step):
        to = lax.rem(replica + step, groups)
        to_chip = lax.div(to, 2)
        src = twice_of(grad_ref, to_chip + 4 - 8 * lax.div(to_chip, 4), lax.rem(to, 2))
        send(src, own_twice, twice_send, twice_recv, {"replica": to}).start()

    pltpu.make_async_copy(twice_of(grad_ref, across, core), own_twice, twice_recv).start()

    await_bytes(held, held_recv)
    plane_small[...] = packed_gram(held[...], groups, rows)

    own_slot = plane_slots.at[(y * rows_x + x) * 2 + core]
    pltpu.make_async_copy(plane_small, own_slot, plane_recv).start()
    far_first = sorted(range(plane), key=lambda step: -hops(step % rows_x, rows_x) - hops(step // rows_x, rows_y))
    for step in far_first:
        for other in (False, True):
            if step > 0 or other:
                to = device(dx=step % rows_x, dy=step // rows_x, other=other)
                send(plane_small, own_slot, plane_send, plane_recv, to).start()
    for step in range(1, groups):
        send_twice(step)
    await_bytes(plane_slots, plane_recv)
    ring_small[...] = jnp.sum(plane_slots[...], axis=0)

    pltpu.make_async_copy(ring_small, ring_slots.at[z], ring_recv).start()
    for step in sorted(range(1, ring), key=lambda step: -hops(step, ring)):
        send(ring_small, ring_slots.at[z], ring_send, ring_recv, device(dz=step)).start()
    await_bytes(ring_slots, ring_recv)
    weights = median_weights(jnp.sum(ring_slots[...], axis=0), weight_ref, groups, entries)

    def pooled(block, width):
        total = jnp.zeros((rows, width), jnp.float32)
        for group in range(groups):
            total += weights[group : group + 1, :1] * block[group * rows : (group + 1) * rows, :].astype(jnp.float32)
        return total

    part_of(out_ref, chip, core)[...] = pooled(held, wide)

    sibling = {"replica": chip * 2 + 1 - core}
    pieces = ((twice, wide - twice, SPREAD), (0, twice, SPREAD_TWICE))
    place = [chip]
    for offset in range(1, chips):
        top = 1 << (offset.bit_length() - 1)
        below = place[offset - top]
        place.append(below + top - 2 * top * lax.rem(lax.div(below, top), 2))

    def piece_of(offset, piece, from_core):
        start, width, _ = pieces[piece]
        return out_ref.at[
            pl.ds(pl.multiple_of(from_core * rows, rows), rows),
            pl.ds(pl.multiple_of(place[offset] * wide + start, LANES), width),
        ]

    def to_chip(child, piece):
        parent = pieces[piece][2][child]
        part = piece_of(parent, piece, core)
        to = {"replica": place[parent ^ child] * 2 + core}
        return send(part, part, chip_send, chip_recv.at[child, piece], to)

    def from_chip(child, piece):
        part = piece_of(child, piece, core)
        return pltpu.make_async_copy(part, part, chip_recv.at[child, piece])

    def to_core(offset, piece):
        part = piece_of(offset, piece, core)
        return send(part, part, core_send, core_recv, sibling)

    def passed_on(offset, piece):
        for child, parent in pieces[piece][2].items():
            if parent == offset:
                to_chip(child, piece).start()

    for piece in range(2):
        passed_on(0, piece)
    for piece in range(2):
        to_core(0, piece).start()
    await_bytes(held_twice, twice_recv)
    twice_of(out_ref, across, core)[...] = pooled(held_twice, twice)
    passed_on(4, 1)
    to_core(4, 1).start()
    for copy in kept:
        copy.wait()
    await_bytes(held.at[pl.ds(0, (groups - 1) * rows), :], held_send)
    await_bytes(plane_slots.at[pl.ds(0, 2 * plane - 1)], plane_send)
    await_bytes(ring_slots.at[pl.ds(0, ring - 1)], ring_send)
    for piece, offset in ARRIVALS:
        from_chip(offset, piece).wait()
        passed_on(offset, piece)
        to_core(offset, piece).start()
    sent = sum(width * len(tree) for _, width, tree in pieces)
    await_bytes(out_ref.at[pl.ds(0, rows), pl.ds(0, sent)], chip_send)
    await_bytes(held_twice.at[pl.ds(0, (groups - 1) * rows), :], twice_send)
    await_bytes(out_ref.at[pl.ds(pl.multiple_of(core * rows, rows), rows), :], core_send)
    await_bytes(out_ref.at[pl.ds(pl.multiple_of((1 - core) * rows, rows), rows), :], core_recv)


def update_kernel(
    median_ref, params_ref, first_ref, second_ref, median_hbm, params_hbm, first_hbm, second_hbm,
    params_new, first_new, second_new, median_sem, sems,
):
    median_copy = pltpu.make_async_copy(median_ref, median_hbm, median_sem)
    median_copy.start()
    rows, width = median_ref.shape
    cut = 8
    copies = []
    for part in range(rows // cut):
        at = pl.ds(part * cut, cut)
        median = median_ref[at, :]
        new_first = beta_first * first_ref[at, :] + (1.0 - beta_first) * median
        new_second = beta_second * second_ref[at, :] + (1.0 - beta_second) * median * median
        first_hat = new_first / (1.0 - beta_first**STEP)
        second_hat = new_second / (1.0 - beta_second**STEP)
        params = params_ref[at, :]
        params_new[at, :] = params - learn_rate * (
            first_hat / (jnp.sqrt(second_hat) + adam_epsilon) + decay_rate * params
        )
        first_new[at, :] = new_first
        second_new[at, :] = new_second
        for kind, (new, hbm) in enumerate(
            ((params_new, params_hbm), (first_new, first_hbm), (second_new, second_hbm))
        ):
            copy = pltpu.make_async_copy(new.at[at, :], hbm.at[at, :], sems.at[part, kind])
            copy.start()
            copies.append(copy)
    for copy in copies:
        copy.wait()
    median_copy.wait()


def body(chips, grid, gradients, replica_weight, params, first_moment, second_moment):
    rows_here, width = gradients.shape[1], gradients.shape[2]
    rows_y, runs, rows_x = grid
    groups, ring = 2 * chips, runs * chips
    entries = rows_here * rows_y * runs * rows_x * width
    rows, wide = rows_here // 2, width // chips
    dma, regular = pltpu.SemaphoreType.DMA, pltpu.SemaphoreType.REGULAR
    whole = jax.ShapeDtypeStruct((rows_here, width), jnp.float32)
    in_hbm = pl.BlockSpec(memory_space=pltpu.HBM)
    in_vmem = pl.BlockSpec(memory_space=pltpu.VMEM)
    small = pltpu.VMEM((2, LANES), jnp.float32)
    inputs = (gradients.reshape(rows_here, width), replica_weight, params, first_moment, second_moment)
    gathered = pl.pallas_call(
        functools.partial(kernel, chips, grid, entries),
        out_shape=(whole,) * 4,
        in_specs=[in_hbm] * 5,
        out_specs=(in_vmem,) * 4,
        scratch_shapes=[
            pltpu.VMEM((rows_here, width), jnp.bfloat16),
            pltpu.SMEM((groups,), jnp.float32),
            pltpu.VMEM((groups * rows, wide), jnp.bfloat16),
            pltpu.VMEM((groups * rows, TWICE_LANES), jnp.bfloat16),
            small, small,
            pltpu.VMEM((2 * rows_x * rows_y, 2, LANES), jnp.float32),
            pltpu.VMEM((ring, 2, LANES), jnp.float32),
            regular((3,)), regular, regular, regular, regular, regular,
            dma, dma, dma((3,)), dma, dma, dma, dma,
            dma, dma, dma, dma,
            dma, dma((chips, 2)), dma, dma,
        ],
        compiler_params=pltpu.CompilerParams(collective_id=0, has_side_effects=True, vmem_limit_bytes=51 * 1024 * 1024),
        name="median_rows",
    )(*(pltpu.with_memory_space_constraint(array, pltpu.HBM) for array in inputs))
    kept = pltpu.VMEM((rows_here, width), jnp.float32)
    return pl.pallas_call(
        update_kernel,
        out_shape=(whole,) * 4,
        in_specs=[in_vmem] * 4,
        out_specs=(in_hbm,) * 4,
        scratch_shapes=[kept, kept, kept, dma, dma((rows_here // 8, 3))],
        compiler_params=pltpu.CompilerParams(vmem_limit_bytes=16 * 1024 * 1024),
        name="update",
    )(*gathered)


def solution(mesh):
    chips = mesh.shape["replica"] // 2
    side = math.isqrt(mesh.shape["fsdp"] // 2)
    return jax.shard_map(
        functools.partial(body, chips, (side, 2, side)),
        mesh=mesh,
        in_specs=(
            P("replica", "fsdp", None),
            P(),
            P("fsdp", None),
            P("fsdp", None),
            P("fsdp", None),
        ),
        out_specs=(P("fsdp", None), P("fsdp", None), P("fsdp", None), P("fsdp", None)),
        check_vma=False,
    )
```

```python
import functools
import math

import jax
import jax.numpy as jnp
from jax import lax
from jax.experimental import pallas as pl
from jax.experimental.pallas import tpu as pltpu
from jax.sharding import PartitionSpec as P

ITERS = 4
STEP = 100

smooth_floor = 0.05
beta_first = 0.9
beta_second = 0.95
learn_rate = 0.001
decay_rate = 0.1
adam_epsilon = 1e-08

MESH = pl.DeviceIdType.MESH
LANES = 128
SPREAD = {4: 0, 2: 0, 1: 0, 3: 0, 6: 4, 5: 4, 7: 4}
SPREAD_TWICE = {1: 0, 2: 0, 3: 0, 5: 4, 6: 4, 7: 4}
TWICE_LANES = 384
ARRIVALS = [(0, 4), (0, 2), (0, 1), (0, 3), (1, 1), (1, 2), (1, 3), (1, 5), (1, 6), (1, 7), (0, 6), (0, 5), (0, 7)]


def packed_gram(block, groups, rows):
    product = lax.dot_general(block, block, (((1,), (1,)), ((), ())), preferred_element_type=jnp.float32)
    size = groups * rows
    row = lax.broadcasted_iota(jnp.int32, (size, size), 0)
    column = lax.broadcasted_iota(jnp.int32, (size, size), 1)
    same = lax.rem(row, rows) == lax.rem(column, rows)
    by_group = jnp.sum(jnp.where(same, product, 0.0).reshape(groups, rows, size), axis=1)
    lane = lax.broadcasted_iota(jnp.int32, (groups, LANES), 1)

    def fold(low, high, step):
        low, high = low + pltpu.roll(low, LANES - step, 1), high + pltpu.roll(high, step, 1)
        return jnp.where(lax.rem(lane[: low.shape[0]], 2 * step) < step, low, high)

    folded = fold(by_group[:, :LANES], by_group[:, LANES:], 8)
    folded = fold(folded[:8], folded[8:], 4)
    folded = fold(folded[:4], folded[4:], 2)
    return fold(folded[:2], folded[2:], 1)


def given_weights(weight_ref, groups):
    sub = lax.broadcasted_iota(jnp.int32, (groups, LANES), 0)
    given = jnp.zeros((groups, LANES), jnp.float32)
    for group in range(groups):
        given = jnp.where(sub == group, weight_ref[group], given)
    return given


def median_weights(packed, given, groups, entries):
    lane = lax.broadcasted_iota(jnp.int32, (groups, LANES), 1)
    sub = lax.broadcasted_iota(jnp.int32, (groups, LANES), 0)
    lane_group = lax.div(lane, 16) + 8 * lax.div(lax.rem(lane, 16), 8)
    here = lax.rem(lane, 8) == lax.div(sub, 2)
    both = jnp.where(lax.rem(sub, 2) == 0, packed[:1], packed[1:])
    gram = jnp.where(here, both, 0.0) * (1.0 / entries)
    own_lane = lane_group == sub
    norm = jnp.sum(jnp.where(own_lane, gram, 0.0), axis=1, keepdims=True)
    weight = given
    for iteration in range(ITERS + 1):
        weight = weight / jnp.sum(weight, axis=0, keepdims=True)
        if iteration == ITERS:
            break
        along_lanes = jnp.sum(jnp.where(own_lane, weight, 0.0), axis=0, keepdims=True)
        product = jnp.sum(gram * along_lanes, axis=1, keepdims=True)
        squared = norm - 2.0 * product + jnp.sum(weight * product, axis=0, keepdims=True)
        weight = given / jnp.maximum(jnp.sqrt(jnp.maximum(squared, 0.0)), smooth_floor)
    return weight


def kernel(
    chips, grid, entries, grad_hbm, weight_hbm, params_hbm, first_hbm, second_hbm,
    out_ref, params_ref, first_ref, second_ref,
    grad_ref, weight_ref, held, held_twice, plane_small, ring_small, plane_slots, ring_slots,
    reached, both_sem, beside_sem, near_row, next_row, far_row,
    grad_sem, weight_sem, copy_sem, held_send, held_recv, twice_send, twice_recv,
    plane_send, plane_recv, ring_send, ring_recv,
    chip_send, chip_recv, core_send, core_recv,
):
    rows_y, runs, rows_x = grid
    groups, plane, ring = 2 * chips, rows_x * rows_y, runs * chips
    replica, fsdp = lax.axis_index("replica"), lax.axis_index("fsdp")
    chip, core = lax.div(replica, 2), lax.rem(replica, 2)
    x, run, y = lax.rem(fsdp, rows_x), lax.rem(lax.div(fsdp, rows_x), runs), lax.div(fsdp, rows_x * runs)
    z = run * chips + chip
    rows = grad_ref.shape[0] // 2
    wide = grad_ref.shape[1] // chips
    twice = held_twice.shape[1]

    def device(dz=0, dy=0, dx=0, other=False):
        to_z = lax.rem(z + dz + ring, ring)
        to_y = lax.rem(y + dy + rows_y, rows_y)
        to_x = lax.rem(x + dx + rows_x, rows_x)
        return {
            "replica": lax.rem(to_z, chips) * 2 + (1 - core if other else core),
            "fsdp": (to_y * runs + lax.div(to_z, chips)) * rows_x + to_x,
        }

    def hops(step, size):
        return min(step, size - step)

    def steps(size):
        return {1: (), 2: (1,)}.get(size, (1, -1))

    def tell(sem, to):
        pl.semaphore_signal(sem, inc=1, device_id=to, device_id_type=MESH)

    def send(src, dst, send_sem, recv_sem, to):
        return pltpu.make_async_remote_copy(
            src_ref=src, dst_ref=dst, send_sem=send_sem, recv_sem=recv_sem, device_id=to, device_id_type=MESH
        )

    def await_bytes(ref, sem):
        pltpu.make_async_copy(ref, ref, sem).wait()

    barrier = pltpu.get_barrier_semaphore()
    greeted = [device(dz=dz, other=other) for dz in (-2, -1, 1, 2) for other in (False, True)]
    greeted += [device(dy=dy) for dy in steps(rows_y)] + [device(dx=dx) for dx in steps(rows_x)]
    greeted += [device(other=True)]
    for to in greeted:
        tell(barrier, to)
    grad_copy = pltpu.make_async_copy(grad_hbm, grad_ref, grad_sem)
    grad_copy.start()
    weight_copy = pltpu.make_async_copy(weight_hbm, weight_ref, weight_sem)
    weight_copy.start()
    pl.semaphore_wait(barrier, len(greeted))

    def part_of(ref, owner_chip, owner_core):
        return ref.at[
            pl.ds(pl.multiple_of(owner_core * rows, rows), rows),
            pl.ds(pl.multiple_of(owner_chip * wide, wide), wide),
        ]

    own_held = held.at[pl.ds(pl.multiple_of(replica * rows, rows), rows), :]

    def send_part(to_chip, to_core):
        to = {"replica": to_chip * 2 + to_core}
        send(part_of(grad_ref, to_chip, to_core), own_held, held_send, held_recv, to).start()

    def send_at(distance, send_one=send_part):
        @pl.when(chip + distance < chips)
        def _():
            send_one(chip + distance, core)
            send_one(chip + distance, 1 - core)

        @pl.when(chip >= distance)
        def _():
            send_one(chip - distance, core)
            send_one(chip - distance, 1 - core)

    def tell_both(stage, through):
        tell(reached.at[stage], device(dz=through))
        tell(reached.at[stage], device(dz=-through))

    tell_both(0, 2)
    grad_copy.wait()
    send_part(chip, 1 - core)
    pltpu.make_async_copy(part_of(grad_ref, chip, core), own_held, held_recv).start()
    send_at(1)
    send_at(2)
    pl.semaphore_wait(reached.at[0], 2)
    tell_both(1, 3)
    send_at(3)
    send_at(4)
    pl.semaphore_wait(reached.at[1], 2)
    tell_both(2, 1)
    send_at(5)
    send_at(6)
    send_at(7)

    for dx in steps(rows_x):
        tell(both_sem, device(dx=dx))
    if rows_x > 1:
        pl.semaphore_wait(both_sem, len(steps(rows_x)))
    if rows_x > 2:
        tell(beside_sem, device(dx=1))
        pl.semaphore_wait(beside_sem, 1)
    for dy in steps(rows_y):
        tell(near_row if dy == 1 else next_row, device(dy=dy))
    for dy in steps(rows_y):
        pl.semaphore_wait(near_row if dy == 1 else next_row, 1)
    if rows_y > 2:
        tell(far_row, device(dy=1))
        pl.semaphore_wait(far_row, 1)
    pl.semaphore_wait(reached.at[2], 2)

    kept = [
        pltpu.make_async_copy(params_hbm, params_ref, copy_sem.at[0]),
        pltpu.make_async_copy(first_hbm, first_ref, copy_sem.at[1]),
        pltpu.make_async_copy(second_hbm, second_ref, copy_sem.at[2]),
    ]
    for copy in kept:
        copy.start()
    weight_copy.wait()

    across = chip + 4 - 8 * lax.div(chip, 4)
    own_twice = held_twice.at[pl.ds(pl.multiple_of(replica * rows, rows), rows), :]

    def twice_of(ref, owner_chip, owner_core):
        return ref.at[
            pl.ds(pl.multiple_of(owner_core * rows, rows), rows),
            pl.ds(pl.multiple_of(owner_chip * wide, wide), twice),
        ]

    def send_twice(to_chip, to_core):
        src = twice_of(grad_ref, to_chip + 4 - 8 * lax.div(to_chip, 4), to_core)
        send(src, own_twice, twice_send, twice_recv, {"replica": to_chip * 2 + to_core}).start()

    pltpu.make_async_copy(twice_of(grad_ref, across, core), own_twice, twice_recv).start()

    await_bytes(held, held_recv)
    plane_small[...] = packed_gram(held[...], groups, rows)

    own_slot = plane_slots.at[(y * rows_x + x) * 2 + core]
    pltpu.make_async_copy(plane_small, own_slot, plane_recv).start()
    far_first = sorted(range(plane), key=lambda step: -hops(step % rows_x, rows_x) - hops(step // rows_x, rows_y))
    for step in far_first:
        for other in (False, True):
            if step > 0 or other:
                to = device(dx=step % rows_x, dy=step // rows_x, other=other)
                send(plane_small, own_slot, plane_send, plane_recv, to).start()
    send_twice(chip, 1 - core)
    for distance in range(1, chips):
        send_at(distance, send_twice)
    await_bytes(plane_slots, plane_recv)
    ring_small[...] = jnp.sum(plane_slots[...], axis=0)

    pltpu.make_async_copy(ring_small, ring_slots.at[z], ring_recv).start()
    for step in sorted(range(1, ring), key=lambda step: -hops(step, ring)):
        send(ring_small, ring_slots.at[z], ring_send, ring_recv, device(dz=step)).start()
    given = given_weights(weight_ref, groups)
    await_bytes(ring_slots, ring_recv)
    weights = median_weights(jnp.sum(ring_slots[...], axis=0), given, groups, entries)

    def pooled(block, start, width):
        total = jnp.zeros((rows, width), jnp.float32)
        for group in range(groups):
            part = block[group * rows : (group + 1) * rows, start : start + width]
            total += weights[group : group + 1, :1] * part.astype(jnp.float32)
        return total

    sibling = {"replica": chip * 2 + 1 - core}
    pieces = ((twice, wide - twice, SPREAD), (0, twice, SPREAD_TWICE))
    place = [chip]
    for offset in range(1, chips):
        top = 1 << (offset.bit_length() - 1)
        below = place[offset - top]
        place.append(below + top - 2 * top * lax.rem(lax.div(below, top), 2))

    def piece_of(offset, piece, from_core):
        start, width, _ = pieces[piece]
        return out_ref.at[
            pl.ds(pl.multiple_of(from_core * rows, rows), rows),
            pl.ds(pl.multiple_of(place[offset] * wide + start, LANES), width),
        ]

    def to_chip(child, piece):
        parent = pieces[piece][2][child]
        part = piece_of(parent, piece, core)
        to = {"replica": place[parent ^ child] * 2 + core}
        return send(part, part, chip_send, chip_recv.at[child, piece], to)

    def from_chip(child, piece):
        part = piece_of(child, piece, core)
        return pltpu.make_async_copy(part, part, chip_recv.at[child, piece])

    def to_core(offset, piece):
        part = piece_of(offset, piece, core)
        return send(part, part, core_send, core_recv, sibling)

    def passed_on(offset, piece):
        for child, parent in pieces[piece][2].items():
            if parent == offset:
                to_chip(child, piece).start()

    for piece, (start, width, _) in enumerate(pieces):
        piece_of(0, piece, core)[...] = pooled(held, start, width)
        passed_on(0, piece)
    for piece in range(2):
        to_core(0, piece).start()
    await_bytes(held_twice, twice_recv)
    twice_of(out_ref, across, core)[...] = pooled(held_twice, 0, twice)
    passed_on(4, 1)
    to_core(4, 1).start()
    for copy in kept:
        copy.wait()
    await_bytes(held.at[pl.ds(0, (groups - 1) * rows), :], held_send)
    await_bytes(plane_slots.at[pl.ds(0, 2 * plane - 1)], plane_send)
    await_bytes(ring_slots.at[pl.ds(0, ring - 1)], ring_send)
    for piece, offset in ARRIVALS:
        from_chip(offset, piece).wait()
        passed_on(offset, piece)
        to_core(offset, piece).start()
    sent = sum(width * len(tree) for _, width, tree in pieces)
    await_bytes(out_ref.at[pl.ds(0, rows), pl.ds(0, sent)], chip_send)
    await_bytes(held_twice.at[pl.ds(0, (groups - 1) * rows), :], twice_send)
    await_bytes(out_ref.at[pl.ds(pl.multiple_of(core * rows, rows), rows), :], core_send)
    await_bytes(out_ref.at[pl.ds(pl.multiple_of((1 - core) * rows, rows), rows), :], core_recv)


def update_kernel(
    median_ref, params_ref, first_ref, second_ref, median_hbm, params_hbm, first_hbm, second_hbm,
    params_new, first_new, second_new, median_sem, sems,
):
    median_copy = pltpu.make_async_copy(median_ref, median_hbm, median_sem)
    median_copy.start()
    rows, width = median_ref.shape
    cut = 8
    copies = []
    for part in range(rows // cut):
        at = pl.ds(part * cut, cut)
        median = median_ref[at, :]
        new_first = beta_first * first_ref[at, :] + (1.0 - beta_first) * median
        new_second = beta_second * second_ref[at, :] + (1.0 - beta_second) * median * median
        first_hat = new_first / (1.0 - beta_first**STEP)
        second_hat = new_second / (1.0 - beta_second**STEP)
        params = params_ref[at, :]
        params_new[at, :] = params - learn_rate * (
            first_hat / (jnp.sqrt(second_hat) + adam_epsilon) + decay_rate * params
        )
        first_new[at, :] = new_first
        second_new[at, :] = new_second
        for kind, (new, hbm) in enumerate(
            ((params_new, params_hbm), (first_new, first_hbm), (second_new, second_hbm))
        ):
            copy = pltpu.make_async_copy(new.at[at, :], hbm.at[at, :], sems.at[part, kind])
            copy.start()
            copies.append(copy)
    for copy in copies:
        copy.wait()
    median_copy.wait()


def body(chips, grid, gradients, replica_weight, params, first_moment, second_moment):
    rows_here, width = gradients.shape[1], gradients.shape[2]
    rows_y, runs, rows_x = grid
    groups, ring = 2 * chips, runs * chips
    entries = rows_here * rows_y * runs * rows_x * width
    rows, wide = rows_here // 2, width // chips
    dma, regular = pltpu.SemaphoreType.DMA, pltpu.SemaphoreType.REGULAR
    whole = jax.ShapeDtypeStruct((rows_here, width), jnp.float32)
    in_hbm = pl.BlockSpec(memory_space=pltpu.HBM)
    in_vmem = pl.BlockSpec(memory_space=pltpu.VMEM)
    small = pltpu.VMEM((2, LANES), jnp.float32)
    inputs = (gradients.reshape(rows_here, width), replica_weight, params, first_moment, second_moment)
    gathered = pl.pallas_call(
        functools.partial(kernel, chips, grid, entries),
        out_shape=(whole,) * 4,
        in_specs=[in_hbm] * 5,
        out_specs=(in_vmem,) * 4,
        scratch_shapes=[
            pltpu.VMEM((rows_here, width), jnp.bfloat16),
            pltpu.SMEM((groups,), jnp.float32),
            pltpu.VMEM((groups * rows, wide), jnp.bfloat16),
            pltpu.VMEM((groups * rows, TWICE_LANES), jnp.bfloat16),
            small, small,
            pltpu.VMEM((2 * rows_x * rows_y, 2, LANES), jnp.float32),
            pltpu.VMEM((ring, 2, LANES), jnp.float32),
            regular((3,)), regular, regular, regular, regular, regular,
            dma, dma, dma((3,)), dma, dma, dma, dma,
            dma, dma, dma, dma,
            dma, dma((chips, 2)), dma, dma,
        ],
        compiler_params=pltpu.CompilerParams(collective_id=0, has_side_effects=True, vmem_limit_bytes=51 * 1024 * 1024),
        name="median_rows",
    )(*(pltpu.with_memory_space_constraint(array, pltpu.HBM) for array in inputs))
    kept = pltpu.VMEM((rows_here, width), jnp.float32)
    return pl.pallas_call(
        update_kernel,
        out_shape=(whole,) * 4,
        in_specs=[in_vmem] * 4,
        out_specs=(in_hbm,) * 4,
        scratch_shapes=[kept, kept, kept, dma, dma((rows_here // 8, 3))],
        compiler_params=pltpu.CompilerParams(vmem_limit_bytes=16 * 1024 * 1024),
        name="update",
    )(*gathered)


def solution(mesh):
    chips = mesh.shape["replica"] // 2
    side = math.isqrt(mesh.shape["fsdp"] // 2)
    return jax.shard_map(
        functools.partial(body, chips, (side, 2, side)),
        mesh=mesh,
        in_specs=(
            P("replica", "fsdp", None),
            P(),
            P("fsdp", None),
            P("fsdp", None),
            P("fsdp", None),
        ),
        out_specs=(P("fsdp", None), P("fsdp", None), P("fsdp", None), P("fsdp", None)),
        check_vma=False,
    )
```
